32 devices in a mesh: lon: 8 (over y, x, core), lat: 4 (over z).
Axes of the slice: x: 2, y: 2, z: 4, core: 2. Of those that a mesh axis runs over, the one named last changes fastest.
Arguments:
- control: float32 [4, 137, 32, 1024], P(None, None, 'lat', 'lon'), may hold values from -6 to 6
- smoothing: float32 [4, 137, 32, 1024], P(None, None, 'lat', 'lon'), may hold values from 0.45 to 1, as said below
- lat_taps: float32 [4, 5, 32], P(None, None, 'lat'), may hold values from 0.1 to 0.6
- vert_corr: float32 [4, 137, 137], replicated, may hold values from -0.5 to 1.5
- obs_cell: int32 [32, 32, 128], P(('lon', 'lat')), may hold values from 0 to 1023
- obs_field: int32 [32, 32], P(('lon', 'lat')), may hold values from 0 to 3
- obs_count: int32 [32, 32], P(('lon', 'lat')), may hold values from 1 to 128, as said below
- obs_owner: int32 [32, 32], P(('lon', 'lat')), may hold values from 0 to 31, as said below
- obs_jacobian: bfloat16 [32, 137, 32, 128], P(('lon', 'lat')), may hold values from -1 to 1
- obs_value: bfloat16 [32, 32, 128], P(('lon', 'lat')), may hold values from -6 to 6
- obs_precision: bfloat16 [32, 32, 128], P(('lon', 'lat')), may hold values from 0.29882812 to 3
Outputs:
- gradient: float32 [4, 137, 32, 1024], P(None, None, 'lat', 'lon')
- obs_residual: float32 [32, 32, 128], P(('lon', 'lat'))
The draws below stay inside these ranges and needn't reach their ends.
Inputs may be any that keep to these rules, and one draw needn't show every extreme that they name: `smoothing`: each coefficient is positive and below 1. `obs_count`: slots of a block at or past its count are empty; on every device some block has all 128 slots live. `obs_owner`: on each device every owner index names exactly 1 of the 32 blocks.
All inputs are finite; a program needn't handle non-finite values.
Results may differ from the reference program's by a relative error of at most 0.0029.
Values may be sent and summed in bfloat16 or wider, within the bound.
No kernel may reach another device: no remote copies, remote signals or barrier semaphores. Data moves between devices by JAX's collectives and lax.ppermute only.
A program may use at most 192 MiB of HBM per device.

```python
import math
import jax
import jax.numpy as jnp
from jax import lax

STATE_VARIABLES = 4
STACK_HEIGHT = 137
HALO = 2
TAPS = 5
LAT_DEV = 8
LON_DEV = 128
SLOTS = 128
BLK_PEER = 1
OWNERS = 32
BLOCKS = 32
CELLS = 1024
MERIDIAN_SPAN = 32
ZONAL_SPAN = 1024
N_LAT = 4


def draw_smoothing(key, part):
    generator_seeds = jax.random.split(key, 4)
    lowest = math.log(0.3 / ZONAL_SPAN)
    highest = math.log(1.0 / 35.0)
    filter_coefficients = jnp.exp(jax.random.uniform(generator_seeds[0], (STATE_VARIABLES, STACK_HEIGHT, MERIDIAN_SPAN, 1), jnp.float32, lowest, highest))
    unsmoothed_grid = jax.random.uniform(generator_seeds[1], (STATE_VARIABLES, STACK_HEIGHT, MERIDIAN_SPAN, ZONAL_SPAN), jnp.float32, 0.6, 1.6)
    segment_batches = jax.random.uniform(generator_seeds[2], (STATE_VARIABLES, STACK_HEIGHT, MERIDIAN_SPAN, ZONAL_SPAN), jnp.float32) < 3.0 / ZONAL_SPAN
    boundary_indices = jax.random.uniform(generator_seeds[3], (STATE_VARIABLES, STACK_HEIGHT, MERIDIAN_SPAN, ZONAL_SPAN), jnp.float32, 0.5, 0.8)
    return jnp.exp(-filter_coefficients * unsmoothed_grid) * jnp.where(segment_batches, boundary_indices, 1.0)


def draw_vert_corr(key, part):
    noise = jnp.clip(jax.random.normal(key, (STATE_VARIABLES, STACK_HEIGHT, STACK_HEIGHT), jnp.float32), -4.0, 4.0)
    return jnp.eye(STACK_HEIGHT, dtype=jnp.float32)[None] + noise * (0.5 / math.sqrt(STACK_HEIGHT))


def draw_obs_count(key, part):
    generator_seeds = jax.random.split(key, 3)
    levels = jax.random.randint(generator_seeds[0], (OWNERS, 1), SLOTS // 8, SLOTS + 1)
    lowest = jnp.maximum(levels // 2, 1)
    spread = jax.random.randint(generator_seeds[1], (OWNERS, BLOCKS), 0, 1 << 20) % (levels - lowest + 1)
    counts = lowest + spread
    chosen = jax.random.randint(generator_seeds[2], (OWNERS, 1), 0, BLOCKS)
    return jnp.where(jnp.arange(BLOCKS)[None, :] == chosen, SLOTS, counts).astype(jnp.int32)


def draw_obs_owner(key, part):
    base_row = jnp.arange(BLOCKS, dtype=jnp.int32) % OWNERS
    row_keys = jax.random.split(key, OWNERS)
    return jax.vmap(lambda row_key: jax.random.permutation(row_key, base_row))(row_keys).astype(jnp.int32)


def with_ends(array, rng, least, high):
    index_at = [jax.random.randint(jax.random.fold_in(rng, axis), (), 0, length) for axis, length in enumerate(array.shape)]
    widest = array.shape.index(max(array.shape))
    next_to = index_at[:widest] + [(index_at[widest] + 1) % array.shape[widest]] + index_at[widest + 1:]
    return array.at[tuple(index_at)].set(least).at[tuple(next_to)].set(high)


def shard_levels(stream_key, shape, cuts, least, largest):
    gain, own = 1.0, jax.random.fold_in(stream_key, 6)
    for dim, parts in cuts:
        draws = jnp.exp(jax.random.uniform(jax.random.fold_in(own, dim), (parts,), jnp.float32, least / len(cuts), largest / len(cuts)))
        gain = gain * jnp.repeat(draws, shape[dim] // parts).reshape([-1 if axis == dim else 1 for axis in range(len(shape))])
    return gain


def bell_draw(stream_key, shape, deviation, limit, shards=(), kind=jnp.bfloat16):
    array = jax.random.normal(stream_key, shape, jnp.float32) * deviation
    if len(shards) > 0:
        array = shard_levels(stream_key, shape, shards, -0.22, 0.18) * array
    return jnp.clip(array, min=-limit, max=limit).astype(kind)


def setup_inputs(seed: int = 0) -> dict:
    streams_of = jax.random.split(jax.random.key(seed), 12)
    return {
        "control": bell_draw(streams_of[0], (STATE_VARIABLES, STACK_HEIGHT, MERIDIAN_SPAN, ZONAL_SPAN), 1.0, 6.0, ((2, 4), (3, 8)), jnp.float32),
        "smoothing": draw_smoothing(jax.random.fold_in(streams_of[11], 71), 0),
        "lat_taps": jnp.clip(0.1 + 0.5 * jax.random.uniform(streams_of[2], (STATE_VARIABLES, TAPS, MERIDIAN_SPAN), jnp.float32) ** shard_levels(streams_of[2], (STATE_VARIABLES, TAPS, MERIDIAN_SPAN), ((2, 4),), -0.2, 0.2), 0.1, 0.6),
        "vert_corr": draw_vert_corr(jax.random.fold_in(streams_of[11], 71), 0),
        "obs_cell": with_ends(jax.random.randint(streams_of[4], (OWNERS, BLOCKS, SLOTS), 0, CELLS), jax.random.fold_in(streams_of[4], 1), 0, CELLS - 1).astype(jnp.int32),
        "obs_field": with_ends(jax.random.randint(streams_of[5], (OWNERS, BLOCKS), 0, STATE_VARIABLES), jax.random.fold_in(streams_of[5], 1), 0, STATE_VARIABLES - 1).astype(jnp.int32),
        "obs_count": draw_obs_count(jax.random.fold_in(streams_of[11], 71), 0),
        "obs_owner": draw_obs_owner(jax.random.fold_in(streams_of[11], 71), 0),
        "obs_jacobian": bell_draw(streams_of[8], (OWNERS, STACK_HEIGHT, BLOCKS, SLOTS), (STACK_HEIGHT // 4) ** -0.5, 1.0, ((0, 32),)),
        "obs_value": bell_draw(streams_of[9], (OWNERS, BLOCKS, SLOTS), 1.0, 6.0, ((0, 32),)),
        "obs_precision": jnp.clip(jnp.exp(math.log(3.0) - 2.306499 * jax.random.uniform(streams_of[10], (OWNERS, BLOCKS, SLOTS), jnp.float32) ** shard_levels(streams_of[10], (OWNERS, BLOCKS, SLOTS), ((0, 32),), -0.2, 0.2)), 0.29882812, 3.0).astype(jnp.bfloat16),
    }


def pair_combine(earlier, later):
    return (earlier[0] * later[0], later[0] * earlier[1] + later[1])

def periodic_line(damping, source, eastward):
    if not eastward:
        damping = jnp.flip(damping, -1)
        source = jnp.flip(source, -1)
    product, states = lax.associative_scan(pair_combine, (damping, source), axis=damping.ndim - 1)
    start_state = states[..., -1:] / (1.0 - product[..., -1:])
    inclusive = states + product * start_state
    exclusive = jnp.concatenate([start_state, inclusive[..., :-1]], axis=-1)
    if not eastward:
        inclusive = jnp.flip(inclusive, -1)
        exclusive = jnp.flip(exclusive, -1)
    return (inclusive, exclusive)

def forward_field(packed):
    control_part, damping, taps, vertical = packed
    scaling = jnp.sqrt((1.0 - damping) * (1.0 + damping))
    eastern = periodic_line(damping, scaling * control_part, True)[0]
    western = periodic_line(damping, scaling * eastern, False)[0]
    padded = jnp.pad(western, ((0, 0), (HALO, HALO), (0, 0)))
    mixed = jnp.zeros_like(western)
    for offset in range(2 * HALO + 1):
        mixed = mixed + taps[offset][None, :, None] * padded[:, offset:offset + MERIDIAN_SPAN, :]
    return jnp.einsum('kl,lji->kji', vertical, mixed, precision=lax.Precision.HIGHEST)

def adjoint_field(packed):
    forcing_part, damping, taps, vertical = packed
    scaling = jnp.sqrt((1.0 - damping) * (1.0 + damping))
    lifted = jnp.einsum('lk,lji->kji', vertical, forcing_part, precision=lax.Precision.HIGHEST)
    spread = jnp.zeros_like(lifted)
    for offset in range(2 * HALO + 1):
        weighted = jnp.pad(taps[offset][None, :, None] * lifted, ((0, 0), (HALO, HALO), (0, 0)))
        spread = spread + weighted[:, 2 * HALO - offset:2 * HALO - offset + MERIDIAN_SPAN, :]
    eastern = periodic_line(damping, damping * spread, True)[1]
    passed = scaling * (spread + eastern)
    western = periodic_line(damping, damping * passed, False)[1]
    return scaling * (passed + western)

def reference(control, smoothing, lat_taps, vert_corr, obs_cell, obs_field, obs_count, obs_owner, obs_jacobian, obs_value, obs_precision):
    state = lax.map(forward_field, (control, smoothing, lat_taps, vert_corr))
    owners = jnp.arange(OWNERS, dtype=jnp.int32)
    grid_lat = (owners % N_LAT * LAT_DEV)[:, None, None] + obs_cell // LON_DEV
    grid_lon = (owners // N_LAT * LON_DEV)[:, None, None] + obs_cell % LON_DEV
    field_index = jnp.broadcast_to(obs_field[:, :, None], obs_cell.shape)
    live_slots = jnp.arange(SLOTS, dtype=jnp.int32)[None, None, :] < obs_count[:, :, None]
    columns = jnp.moveaxis(state, 1, -1)[field_index, grid_lat, grid_lon]
    columns = jnp.where(live_slots[..., None], columns, 0.0).astype(jnp.bfloat16)
    columns = jnp.transpose(columns, (0, 1, 3, 2))
    onehot = (obs_owner[:, :, None] == owners[None, None, :]).astype(jnp.int32)
    earlier = lax.optimization_barrier(jnp.sum((jnp.cumsum(onehot, axis=1) - onehot) * onehot, axis=2))
    place = (owners[:, None] * BLK_PEER + earlier).astype(jnp.int32)
    received_values = jnp.zeros((OWNERS, BLOCKS, STACK_HEIGHT, SLOTS), jnp.bfloat16).at[obs_owner, place].set(columns)
    radiance_jacobian = jnp.transpose(obs_jacobian, (0, 2, 1, 3)).astype(jnp.float32)
    model_estimate = lax.optimization_barrier(jnp.sum(radiance_jacobian * received_values.astype(jnp.float32), axis=2))
    obs_residual = obs_precision.astype(jnp.float32) * (model_estimate - obs_value.astype(jnp.float32))
    adjoint_columns = (radiance_jacobian * obs_residual[:, :, None, :]).astype(jnp.bfloat16)
    returned = adjoint_columns[obs_owner, place].astype(jnp.float32)
    returned = jnp.where(live_slots[:, :, None, :], returned, 0.0)
    spread = jnp.zeros((STATE_VARIABLES, MERIDIAN_SPAN, ZONAL_SPAN, STACK_HEIGHT), jnp.float32).at[field_index, grid_lat, grid_lon].add(jnp.transpose(returned, (0, 1, 3, 2)))
    forcing = jnp.moveaxis(spread, -1, 1)
    gradient = control + lax.map(adjoint_field, (forcing, smoothing, lat_taps, vert_corr))
    return (gradient, obs_residual)
```

```python
import functools

import jax
import jax.numpy as jnp
from jax import lax
from jax.experimental import pallas as pl
from jax.experimental.pallas import tpu as pltpu
from jax.sharding import PartitionSpec as P

LANES = 128
HALO = 2
BF = jnp.bfloat16
F32 = jnp.float32
NT = (((1,), (1,)), ((), ()))
VMEM = pl.BlockSpec(memory_space=pltpu.VMEM)
SMEM = pl.BlockSpec(memory_space=pltpu.SMEM)


def params(mib):
    return pltpu.CompilerParams(vmem_limit_bytes=mib * 1024 * 1024)


def sds(shape, dtype=F32):
    return jax.ShapeDtypeStruct(shape, dtype)


def split(x):
    high = x.astype(BF)
    return high, (x - high.astype(F32)).astype(BF)


def step_rows(i, per):
    return pl.ds(pl.multiple_of(i * per, 8), per)


def solve_sectors(me, products, ends, cross, backs):
    count = len(products)
    whole, state = products[0], ends[0]
    for s in range(1, count):
        state = products[s] * state + ends[s]
        whole = whole * products[s]
    gap = 1.0 - whole
    east = state / gap
    east_in = jnp.zeros_like(east)
    turned = []
    for s in range(count):
        east_in = jnp.where(me == s, east, east_in)
        turned.append(backs[s] + cross[s] * east)
        east = products[s] * east + ends[s]
    state = turned[count - 1]
    for s in range(count - 2, -1, -1):
        state = products[s] * state + turned[s]
    west = state / gap
    west_in = jnp.zeros_like(west)
    for s in range(count - 1, -1, -1):
        west_in = jnp.where(me == s, west, west_in)
        west = products[s] * west + turned[s]
    return east_in, west_in


def to_lines(src, dst, extra, fields, levels, rows):
    per = (fields + 1) * rows
    over, room = levels - LANES, LANES // fields
    extra[...] = jnp.zeros_like(extra)
    for j in range(rows):
        for f in range(fields):
            tile = src[pl.ds(f * levels * rows + j, LANES, stride=rows), :]
            dst[pl.ds(f * rows + j, LANES, stride=per), :] = tile.T
            extra[j, pl.ds(f * room, over), :] = src[
                pl.ds((f * levels + LANES) * rows + j, over, stride=rows), :
            ]
        dst[pl.ds(fields * rows + j, LANES, stride=per), :] = extra[j].T


def filter_kernel(
    fields, levels, rows, control, smoothing,
    a_t, g_t, w0_t, w1_t, s_t, gq_t, gp_t, ends, x_t, e_t, pe_t, extra,
):
    per = (fields + 1) * rows
    to_lines(smoothing, a_t, extra, fields, levels, rows)
    to_lines(control, x_t, extra, fields, levels, rows)

    def east(i, carry):
        e, p = carry
        at = step_rows(i, per)
        a = a_t[at, :]
        g = jnp.sqrt((1.0 - a) * (1.0 + a))
        g_t[at, :] = g
        pe_t[at, :] = p
        e = a * e + g * x_t[at, :]
        e_t[at, :] = e
        return e, p * a

    zero = jnp.zeros((per, LANES), F32)
    one = jnp.ones((per, LANES), F32)
    e, p = lax.fori_loop(0, LANES, east, (zero, one), unroll=4)

    def west(k, carry):
        w0, w1, s = carry
        at = step_rows(LANES - 1 - k, per)
        a, g = a_t[at, :], g_t[at, :]
        w0 = a * w0 + g * e_t[at, :]
        t = w1 + g * pe_t[at, :]
        gq_t[at, :] = g * t
        w1 = a * t
        gp_t[at, :] = g * s
        s = a * s
        w0_t[at, :] = w0
        w1_t[at, :] = w1
        s_t[at, :] = s
        return w0, w1, s

    w0, w1, _ = lax.fori_loop(0, LANES, west, (zero, zero, one), unroll=4)
    ends[0] = p
    ends[1] = e
    ends[2] = w0
    ends[3] = w1


def pack_halo(src, low, high, fields, rows):
    per = (fields + 1) * rows
    for b in range(fields + 1):
        for j in range(HALO):
            low[b, j] = src[pl.ds(b * rows + j, LANES, stride=per), :].astype(BF)
            high[b, j] = src[pl.ds(b * rows + rows - HALO + j, LANES, stride=per), :].astype(BF)


def unpack_halo(low, high, dst, fields, rows):
    per = (fields + 1) * rows
    for b in range(fields + 1):
        for j in range(HALO):
            dst[pl.ds(b * rows + j, LANES, stride=per), :] = low[b, j].astype(F32)
            dst[pl.ds(b * rows + rows - HALO + j, LANES, stride=per), :] = high[b, j].astype(F32)


def western_kernel(fields, rows, count, me, gathered, w0_t, w1_t, s_t, western, low, high):
    per = (fields + 1) * rows
    part = [[gathered[s, q] for s in range(count)] for q in range(4)]
    east_in, west_in = solve_sectors(me[0], part[0], part[1], part[3], part[2])

    def one(i, _):
        at = step_rows(i, per)
        western[at, :] = w0_t[at, :] + w1_t[at, :] * east_in + s_t[at, :] * west_in
        return 0

    lax.fori_loop(0, LANES, one, 0, unroll=8)
    pack_halo(western, low, high, fields, rows)


def state_kernel(fields, rows, western, low, high, taps, vert, state, halo, mh, ml):
    blocks = fields + 1
    per = blocks * rows
    unpack_halo(low, high, halo, fields, rows)
    tap = [taps[t] for t in range(2 * HALO + 1)]
    row = lax.broadcasted_iota(jnp.int32, (blocks, rows, LANES), 1)

    def mix(i):
        at = step_rows(i, per)
        w = western[at, :].reshape(blocks, rows, LANES)
        h = halo[at, :].reshape(blocks, rows, LANES)
        total = tap[HALO] * w
        for s in range(1, HALO + 1):
            total += tap[HALO + s] * pltpu.roll(jnp.where(row < s, h, w), rows - s, 1)
            total += tap[HALO - s] * pltpu.roll(jnp.where(row >= rows - s, h, w), s, 1)
        return total

    def pair(k, _):
        m = jnp.concatenate([mix(2 * k), mix(2 * k + 1)], axis=1)
        high_part, low_part = split(m)
        at = pl.ds(pl.multiple_of(k * 2 * rows, 16), 2 * rows)
        mh[:, at, :] = high_part
        ml[:, at, :] = low_part
        return 0

    lax.fori_loop(0, LANES // 2, pair, 0, unroll=2)
    for f in range(fields):
        vh, vl = split(vert[f])
        xh = jnp.concatenate([mh[f], mh[fields]], axis=1)
        xl = jnp.concatenate([ml[f], ml[fields]], axis=1)
        out = lax.dot_general(vh, xh, NT, preferred_element_type=F32)
        out += lax.dot_general(vh, xl, NT, preferred_element_type=F32)
        out += lax.dot_general(vl, xh, NT, preferred_element_type=F32)
        state[f] = out.astype(BF)


def obs_kernel(
    fields, levels, rows, field, owner, cells, state, jacobian, taps, vert,
    residual, spread, low, high, order, number, acc, lift, outward,
):
    blocks = fields + 1
    per = blocks * rows
    total = field.shape[0]
    sites = rows * LANES
    for f in range(fields):
        number[f] = 0

    def place(k, _):
        f = field[k]
        n = number[f]
        order[f * total + n] = k
        number[f] = n + 1
        return 0

    lax.fori_loop(0, total, place, 0)
    site = lax.broadcasted_iota(jnp.int32, (sites, 2 * LANES), 0)

    for f in range(fields):
        acc[...] = jnp.zeros_like(acc)
        found = number[f]

        def two(p, _):
            k0 = order[f * total + 2 * p]
            second = 2 * p + 1 < found
            k1 = jnp.where(second, order[f * total + jnp.where(second, 2 * p + 1, 0)], k0)
            c0 = cells[pl.ds(k0, 1), :]
            c1 = jnp.where(second, cells[pl.ds(k1, 1), :], -1)
            onehot = (site == jnp.concatenate([c0, c1], axis=1)).astype(F32).astype(BF)
            o0, o1 = owner[k0], owner[k1]
            j = jnp.concatenate([jacobian[o0], jacobian[o1]], axis=1).astype(F32)
            columns = jnp.dot(state[f], onehot, preferred_element_type=F32)
            model = jnp.sum(j * columns, axis=0, keepdims=True)
            value, precision = j[levels : levels + 1], j[levels + 1 : levels + 2]
            res = precision * (model - value)
            residual[pl.ds(o0, 1), :] = res[:, :LANES]

            @pl.when(second)
            def _():
                residual[pl.ds(o1, 1), :] = res[:, LANES:]

            adjoint = (j * res).astype(BF)
            acc[...] += lax.dot_general(onehot, adjoint, NT, preferred_element_type=F32)
            return 0

        lax.fori_loop(0, (found + 1) // 2, two, 0)
        vh, vl = split(vert[f])
        fh, fl = split(acc[...])
        out = jnp.dot(fh, vh, preferred_element_type=F32)
        out += jnp.dot(fl, vh, preferred_element_type=F32)
        out += jnp.dot(fh, vl, preferred_element_type=F32)
        lift[f] = out[:, :LANES]
        if f == 0:
            lift[fields] = out[:, LANES:]
        else:
            lift[fields] += out[:, LANES:]

    tap = [taps[t] for t in range(2 * HALO + 1)]
    row = lax.broadcasted_iota(jnp.int32, (blocks, rows, LANES), 1)

    def one(i, _):
        x = lift[:, pl.ds(pl.multiple_of(i * rows, 8), rows), :]
        inside = tap[HALO] * x
        beyond = jnp.zeros_like(inside)
        for s in range(1, HALO + 1):
            up = pltpu.roll(tap[HALO - s] * x, rows - s, 1)
            down = pltpu.roll(tap[HALO + s] * x, s, 1)
            up_out, down_out = row >= rows - s, row < s
            inside += jnp.where(up_out, 0.0, up) + jnp.where(down_out, 0.0, down)
            beyond += jnp.where(up_out, up, 0.0) + jnp.where(down_out, down, 0.0)
        at = step_rows(i, per)
        spread[at, :] = inside.reshape(per, LANES)
        outward[at, :] = beyond.reshape(per, LANES)
        return 0

    lax.fori_loop(0, LANES, one, 0, unroll=2)
    pack_halo(outward, low, high, fields, rows)


def adjoint_kernel(fields, rows, spread, low, high, a_t, g_t, u_t, ends, halo, pass_t):
    per = (fields + 1) * rows
    unpack_halo(low, high, halo, fields, rows)
    row = lax.broadcasted_iota(jnp.int32, (per, LANES), 0) % rows
    edge = (row < HALO) | (row >= rows - HALO)

    def east(i, q):
        at = step_rows(i, per)
        t = spread[at, :] + jnp.where(edge, halo[at, :], 0.0) + q
        pass_t[at, :] = g_t[at, :] * t
        return a_t[at, :] * t

    zero = jnp.zeros((per, LANES), F32)
    ends[0] = lax.fori_loop(0, LANES, east, zero, unroll=4)

    def west(k, p):
        at = step_rows(LANES - 1 - k, per)
        t = pass_t[at, :] + p
        u_t[at, :] = g_t[at, :] * t
        return a_t[at, :] * t

    ends[1] = lax.fori_loop(0, LANES, west, zero, unroll=4)


def gradient_kernel(
    fields, levels, rows, count, me, before, gathered, u_t, gq_t, gp_t, control, gradient, full
):
    per = (fields + 1) * rows
    over, room = levels - LANES, LANES // fields
    east_in, west_in = solve_sectors(
        me[0],
        [before[s, 0] for s in range(count)],
        [gathered[s, 0] for s in range(count)],
        [before[s, 3] for s in range(count)],
        [gathered[s, 1] for s in range(count)],
    )

    def one(i, _):
        at = step_rows(i, per)
        full[at, :] = u_t[at, :] + gq_t[at, :] * east_in + gp_t[at, :] * west_in
        return 0

    lax.fori_loop(0, LANES, one, 0, unroll=8)
    for j in range(rows):
        for f in range(fields):
            at = pl.ds(f * levels * rows + j, LANES, stride=rows)
            tile = full[pl.ds(f * rows + j, LANES, stride=per), :].T
            gradient[at, :] = control[at, :] + tile
        rest = full[pl.ds(fields * rows + j, LANES, stride=per), :].T
        for f in range(fields):
            at = pl.ds((f * levels + LANES) * rows + j, over, stride=rows)
            gradient[at, :] = control[at, :] + rest[f * room : f * room + over]


def local(
    control, smoothing, lat_taps, vert_corr, obs_cell, obs_field, obs_count, obs_owner,
    obs_jacobian, obs_value, obs_precision,
):
    fields, levels, rows, longitudes = control.shape
    blocks = fields + 1
    per = blocks * rows
    over, room = levels - LANES, LANES // fields
    count = lax.axis_size("lon")
    both = ("lon", "lat")
    total, slots = obs_cell.shape[1:]
    padded = -(-(levels + 2) // 16) * 16
    lines = longitudes * per
    line = sds((lines, LANES))

    spare = jnp.zeros((padded - levels - 2, total, slots), BF)
    sent = jnp.concatenate([obs_jacobian[0], obs_value, obs_precision, spare], axis=0)
    jacobian = lax.all_to_all(
        jnp.transpose(sent, (1, 0, 2)), both, split_axis=0, concat_axis=0, tiled=True
    )

    me = lax.axis_index("lon").astype(jnp.int32).reshape(1)
    wide = jnp.broadcast_to(
        jnp.transpose(lat_taps, (1, 0, 2))[..., None], (2 * HALO + 1, fields, rows, LANES)
    )
    rest = jnp.repeat(jnp.transpose(lat_taps, (1, 2, 0)), room, axis=2)[:, None]
    taps = jnp.concatenate([wide, rest], axis=1)
    vert = jnp.zeros((fields, padded, 2 * LANES), F32)
    vert = vert.at[:, :levels, :LANES].set(vert_corr[:, :, :LANES])
    for f in range(fields):
        begin = LANES + f * room
        vert = vert.at[f, :levels, begin : begin + over].set(vert_corr[f, :, LANES:])
    live = jnp.arange(slots, dtype=jnp.int32)[None, :] < obs_count[0][:, None]
    cells = jnp.where(live, obs_cell[0] % LANES * rows + obs_cell[0] // LANES, -1)

    flat_control = control.reshape(fields * levels * rows, longitudes)
    flat_smoothing = smoothing.reshape(fields * levels * rows, longitudes)
    sizes = (fields, levels, rows)
    tiles = pltpu.VMEM((lines, LANES), F32)
    a_t, g_t, w0_t, w1_t, s_t, gq_t, gp_t, ends = pl.pallas_call(
        functools.partial(filter_kernel, *sizes),
        out_shape=[line] * 7 + [sds((4, per, LANES))],
        in_specs=[VMEM] * 2,
        out_specs=[VMEM] * 8,
        scratch_shapes=[tiles] * 3 + [pltpu.VMEM((rows, LANES, LANES), F32)],
        compiler_params=params(40),
        name="filter_local",
    )(flat_control, flat_smoothing)
    gathered = lax.all_gather(ends, "lon")

    halo_shape = sds((blocks, HALO, longitudes, LANES), BF)
    western, low, high = pl.pallas_call(
        functools.partial(western_kernel, fields, rows, count),
        out_shape=[line, halo_shape, halo_shape],
        in_specs=[SMEM] + [VMEM] * 4,
        out_specs=[VMEM] * 3,
        compiler_params=params(24),
        name="western",
    )(me, gathered, w0_t, w1_t, s_t)

    bands = lax.axis_size("lat")
    up = [(i, i + 1) for i in range(bands - 1)]
    down = [(i + 1, i) for i in range(bands - 1)]
    after = lax.ppermute(low, "lat", down)
    before = lax.ppermute(high, "lat", up)
    state = pl.pallas_call(
        functools.partial(state_kernel, fields, rows),
        out_shape=sds((fields, padded, rows * longitudes), BF),
        in_specs=[VMEM] * 5,
        out_specs=VMEM,
        scratch_shapes=[tiles] + [pltpu.VMEM((blocks, rows * longitudes, LANES), BF)] * 2,
        compiler_params=params(32),
        name="state",
    )(western, after, before, taps, vert)

    residual, spread, low, high = pl.pallas_call(
        functools.partial(obs_kernel, *sizes),
        out_shape=[sds((total, slots)), line, halo_shape, halo_shape],
        in_specs=[SMEM] * 2 + [VMEM] * 5,
        out_specs=[VMEM] * 4,
        scratch_shapes=[
            pltpu.SMEM((fields * total + 1,), jnp.int32),
            pltpu.SMEM((fields,), jnp.int32),
            pltpu.VMEM((rows * longitudes, padded), F32),
            pltpu.VMEM((blocks, rows * longitudes, LANES), F32),
            tiles,
        ],
        compiler_params=params(48),
        name="observe",
    )(obs_field[0], obs_owner[0], cells, state, jacobian, taps, vert)
    returned = lax.all_to_all(residual, both, split_axis=0, concat_axis=0, tiled=True)

    from_before = lax.ppermute(low, "lat", up)
    from_after = lax.ppermute(high, "lat", down)
    u_t, ends = pl.pallas_call(
        functools.partial(adjoint_kernel, fields, rows),
        out_shape=[line, sds((2, per, LANES))],
        in_specs=[VMEM] * 5,
        out_specs=[VMEM] * 2,
        scratch_shapes=[tiles] * 2,
        compiler_params=params(24),
        name="adjoint_local",
    )(spread, from_before, from_after, a_t, g_t)
    gathered_back = lax.all_gather(ends, "lon")
    gradient = pl.pallas_call(
        functools.partial(gradient_kernel, *sizes, count),
        out_shape=sds(flat_control.shape),
        in_specs=[SMEM] + [VMEM] * 6,
        out_specs=VMEM,
        scratch_shapes=[tiles],
        compiler_params=params(24),
        name="gradient",
    )(me, gathered, gathered_back, u_t, gq_t, gp_t, flat_control)
    return gradient.reshape(control.shape), returned[None]


def solution(mesh):
    return jax.shard_map(
        local,
        mesh=mesh,
        in_specs=(
            P(None, None, "lat", "lon"),
            P(None, None, "lat", "lon"),
            P(None, None, "lat"),
            P(),
            P(("lon", "lat"), None, None),
            P(("lon", "lat"), None),
            P(("lon", "lat"), None),
            P(("lon", "lat"), None),
            P(("lon", "lat"), None, None, None),
            P(("lon", "lat"), None, None),
            P(("lon", "lat"), None, None),
        ),
        out_specs=(P(None, None, "lat", "lon"), P(("lon", "lat"), None, None)),
        check_vma=False,
    )
```

```python
import functools

import jax
import jax.numpy as jnp
from jax import lax
from jax.experimental import pallas as pl
from jax.experimental.pallas import tpu as pltpu
from jax.sharding import PartitionSpec as P

LANES = 128
HALO = 2
FAR_MIB = 60
CELLS = 256
GROUP = 4
BF = jnp.bfloat16
F32 = jnp.float32
NT = (((1,), (1,)), ((), ()))
TN = (((0,), (0,)), ((), ()))
VMEM = pl.BlockSpec(memory_space=pltpu.VMEM)
SMEM = pl.BlockSpec(memory_space=pltpu.SMEM)
HBM = pl.BlockSpec(memory_space=pltpu.HBM)


def params(mib):
    return pltpu.CompilerParams(vmem_limit_bytes=mib * 1024 * 1024)


def cost(microseconds):
    return pl.CostEstimate(
        flops=0, bytes_accessed=int(microseconds * 3.5e6), transcendentals=0
    )


def sds(shape, dtype=F32):
    return jax.ShapeDtypeStruct(shape, dtype)


def split(x):
    high = x.astype(BF)
    return high, (x - high.astype(F32)).astype(BF)


def step_rows(i, per):
    return pl.ds(pl.multiple_of(i * per, 8), per)


def solve_sectors(me, products, ends, cross, backs):
    count = len(products)
    whole, state = products[0], ends[0]
    for s in range(1, count):
        state = products[s] * state + ends[s]
        whole = whole * products[s]
    gap = 1.0 - whole
    east = state / gap
    east_in = jnp.zeros_like(east)
    turned = []
    for s in range(count):
        east_in = jnp.where(me == s, east, east_in)
        turned.append(backs[s] + cross[s] * east)
        east = products[s] * east + ends[s]
    state = turned[count - 1]
    for s in range(count - 2, -1, -1):
        state = products[s] * state + turned[s]
    west = state / gap
    west_in = jnp.zeros_like(west)
    for s in range(count - 1, -1, -1):
        west_in = jnp.where(me == s, west, west_in)
        west = products[s] * west + turned[s]
    return east_in, west_in


def fetch(pairs, arrived):
    copies = [pltpu.make_async_copy(a, b, arrived.at[n]) for n, (a, b) in enumerate(pairs)]
    for copy in copies:
        copy.start()
    return copies


def pack_kernel(levels, jacobian, value, precision, sent, held, small, wide, ready, arrived, left):
    blocks, padded = sent.shape[:2]
    chunk = held.shape[2]
    copies = fetch(
        [(value, small.at[0]), (precision, small.at[1])]
        + [
            (jacobian.at[:, pl.ds(c * chunk, chunk)], held.at[c])
            for c in range(blocks // chunk)
        ],
        arrived,
    )
    spare = (padded - levels - 2) * chunk
    wide[pl.ds((levels + 2) * chunk, spare), :] = jnp.zeros((spare, LANES), F32)
    copies[0].wait()
    copies[1].wait()
    leaving = []
    for c in range(blocks // chunk):
        copies[2 + c].wait()

        def put(l, _):
            wide[pl.ds(pl.multiple_of(l * chunk, 8), chunk), :] = held[c, l].astype(F32)
            return 0

        lax.fori_loop(0, levels, put, 0, unroll=8)
        for n in range(2):
            part = small[n, pl.ds(c * chunk, chunk), :].astype(F32)
            wide[pl.ds((levels + n) * chunk, chunk), :] = part
        for k in range(chunk):
            ready[c * chunk + k] = wide[pl.ds(k, padded, stride=chunk), :].astype(BF)
        at = pl.ds(c * chunk, chunk)
        leaving += fetch([(ready.at[at], sent.at[at])], left.at[pl.ds(c, 1)])
    for copy in leaving:
        copy.wait()


def prepare_kernel(fields, levels, rows, vert, lat_taps, both, taps, wide):
    over, room = levels - LANES, LANES // fields
    wide[...] = jnp.zeros_like(wide)
    for f in range(fields):
        v = vert[:, f, :]
        wide[f, :levels, :LANES] = v[:, :LANES]
        begin = LANES + f * room
        wide[f, :levels, begin : begin + over] = v[:, LANES:]
    both[:, :, : 2 * LANES], both[:, :, 2 * LANES :] = split(wide[...])
    diagonal = lax.broadcasted_iota(jnp.int32, (rows, rows), 0) == lax.broadcasted_iota(
        jnp.int32, (rows, rows), 1
    )
    lane = lax.broadcasted_iota(jnp.int32, (rows, LANES), 1) // room
    for t in range(2 * HALO + 1):
        last = jnp.zeros((rows, LANES), F32)
        for f in range(fields):
            line = jnp.broadcast_to(lat_taps[t, f : f + 1, :], (rows, rows))
            column = jnp.sum(jnp.where(diagonal, line, 0.0), axis=1, keepdims=True)
            column = jnp.broadcast_to(column, (rows, LANES))
            taps[t, f] = column
            last = jnp.where(lane == f, column, last)
        taps[t, fields] = last


def filter_kernel(
    fields, levels, rows, control, smoothing,
    a_t, w0_t, w1_t, s_t, ends, control_v, smoothing_v, g_t, x_t, e_t, pe_t, extra, arrived,
):
    per = (fields + 1) * rows
    over, room = levels - LANES, LANES // fields
    pairs = []
    for f in range(fields):
        at = pl.ds(f * levels * rows, levels * rows)
        pairs.append((smoothing.at[at], smoothing_v.at[at]))
        pairs.append((control.at[at], control_v.at[at]))
    copies = fetch(pairs, arrived)
    extra[...] = jnp.zeros_like(extra)
    for f in range(fields):
        for n, (src, dst) in enumerate(((smoothing_v, a_t), (control_v, x_t))):
            copies[2 * f + n].wait()
            for j in range(rows):
                tile = src[pl.ds(f * levels * rows + j, LANES, stride=rows), :]
                dst[pl.ds(f * rows + j, LANES, stride=per), :] = tile.T
                extra[n, j, pl.ds(f * room, over), :] = src[
                    pl.ds((f * levels + LANES) * rows + j, over, stride=rows), :
                ]
    for j in range(rows):
        at = pl.ds(fields * rows + j, LANES, stride=per)
        a_t[at, :] = extra[0, j].T
        x_t[at, :] = extra[1, j].T

    def east(i, carry):
        e, p = carry
        at = step_rows(i, per)
        a = a_t[at, :]
        g = jnp.sqrt((1.0 - a) * (1.0 + a))
        g_t[at, :] = g
        pe_t[at, :] = p
        e = a * e + g * x_t[at, :]
        e_t[at, :] = e
        return e, p * a

    zero = jnp.zeros((per, LANES), F32)
    one = jnp.ones((per, LANES), F32)
    e, p = lax.fori_loop(0, LANES, east, (zero, one), unroll=4)

    def west(k, carry):
        w0, w1, s = carry
        at = step_rows(LANES - 1 - k, per)
        a, g = a_t[at, :], g_t[at, :]
        w0 = a * w0 + g * e_t[at, :]
        w1 = a * (w1 + g * pe_t[at, :])
        s = a * s
        w0_t[at, :] = w0
        w1_t[at, :] = w1
        s_t[at, :] = s
        return w0, w1, s

    w0, w1, _ = lax.fori_loop(0, LANES, west, (zero, zero, one), unroll=4)
    ends[0] = p
    ends[1] = e
    ends[2] = w0
    ends[3] = w1


def edges_kernel(fields, rows, count, gathered, w0_t, w1_t, s_t, low, high, entering):
    per = (fields + 1) * rows
    part = [[gathered[s, q] for s in range(count)] for q in range(4)]
    east_in, west_in = solve_sectors(lax.axis_index("lon"), part[0], part[1], part[3], part[2])
    entering[0] = east_in
    entering[1] = west_in
    for b in range(fields + 1):
        for j in range(HALO):
            to = pl.ds((b * HALO + j) * LANES, LANES)
            for first, dst in ((b * rows, low), (b * rows + rows - HALO, high)):
                n = first + j
                at = pl.ds(n, LANES, stride=per)
                line = w0_t[at, :] + w1_t[at, :] * east_in[n : n + 1]
                dst[to, :] = (line + s_t[at, :] * west_in[n : n + 1]).astype(BF)


def vertical(vert, mixed):
    padded = vert.shape[0]
    v = jnp.concatenate([vert[:, : 2 * LANES], vert[:, 2 * LANES :]], axis=0)
    high, low = split(mixed)
    out = lax.dot_general(v, high, NT, preferred_element_type=F32)
    out = out[:padded] + out[padded:]
    out += lax.dot_general(v[:padded], low, NT, preferred_element_type=F32)
    return out.astype(BF)


def interior_kernel(fields, rows, entering, w0_t, w1_t, s_t, taps, vert, state, partial, western, mixed):
    blocks = fields + 1
    per = blocks * rows
    for n in range(per):
        at = pl.ds(n, LANES, stride=per)
        line = w0_t[at, :] + w1_t[at, :] * entering[0, n : n + 1, :]
        western[n] = line + s_t[at, :] * entering[1, n : n + 1, :]
    for b in range(blocks):
        for j in range(rows):
            total = taps[HALO, b, j : j + 1, :] * western[b * rows + j]
            for t in range(2 * HALO + 1):
                if t != HALO and 0 <= j + t - HALO < rows:
                    total += taps[t, b, j : j + 1, :] * western[b * rows + j + t - HALO]
            if HALO <= j < rows - HALO:
                mixed[b, pl.ds((j - HALO) * LANES, LANES), :] = total
            else:
                partial[b, j if j < HALO else j - rows + 2 * HALO] = total
    for f in range(fields):
        for h in range(state.shape[1]):
            at = pl.ds(h * CELLS, CELLS)
            both = jnp.concatenate([mixed[f, at, :], mixed[fields, at, :]], axis=1)
            state[f, h] = vertical(vert[f], both)


def route_of(delta, bands):
    cyclic = 2 + (delta + bands) % bands
    far = jnp.where(jnp.abs(delta) == bands - 1, 3, cyclic)
    near = jnp.where(delta == 1, 1, jnp.where(delta == -1, 2, 0))
    return jnp.where(jnp.abs(delta) <= 1, near, far)


def observe_kernel(
    fields, levels, rows, bands, field, owner, live, cells,
    inner_far, partial_far, before_far, after_far, taps_far, vert_far, jacobian_far, *rest,
):
    lift_far, low_far, high_far = rest[:3]
    residuals = rest[3 : 2 + bands]
    (
        inner, partial, before, after, taps, vert, jacobian, mixed, outer, lift, low, high,
        route, order, number, acc, arrived, left,
    ) = rest[2 + bands :]
    blocks = fields + 1
    copies = fetch(
        [(after_far, after), (before_far, before), (taps_far, taps), (partial_far, partial)]
        + [(vert_far, vert), (jacobian_far, jacobian), (inner_far, inner)],
        arrived,
    )
    total = field.shape[0]
    padded = vert.shape[1]
    parts = rows * LANES // CELLS
    wide = GROUP * LANES
    sectors = total // bands
    band = lax.axis_index("lat")
    for f in range(fields):
        number[f] = 0

    def place(k, _):
        f = field[k]
        n = number[f]
        order[f * total + n] = k
        number[f] = n + 1
        return 0

    lax.fori_loop(0, total, place, 0)
    route[...] = jnp.zeros_like(route)

    for n in range(4):
        copies[n].wait()

    def beside(src, b, n):
        return src[pl.ds((b * HALO + n) * LANES, LANES), :].astype(F32)

    def tap_of(t, b, j):
        return taps[t, b, j : j + 1, :]

    end = rows - 1
    for b in range(blocks):
        above, below = [beside(before, b, n) for n in range(2)], [beside(after, b, n) for n in range(2)]
        outer_rows = (
            partial[b, 0] + tap_of(0, b, 0) * above[0] + tap_of(1, b, 0) * above[1],
            partial[b, 1] + tap_of(0, b, 1) * above[1],
            partial[b, 2] + tap_of(4, b, end - 1) * below[0],
            partial[b, 3] + tap_of(3, b, end) * below[0] + tap_of(4, b, end) * below[1],
        )
        for n, line in enumerate(outer_rows):
            mixed[b, pl.ds(n * LANES, LANES), :] = line
    copies[4].wait()
    for f in range(fields):
        for h in range(2):
            at = pl.ds(h * CELLS, CELLS)
            both = jnp.concatenate([mixed[f, at, :], mixed[fields, at, :]], axis=1)
            outer[f, h] = vertical(vert[f], both)

    copies[5].wait()
    copies[6].wait()
    site = lax.broadcasted_iota(jnp.int32, (CELLS, wide), 0)
    slot = lax.broadcasted_iota(jnp.int32, (1, LANES), 1)
    leaving = []
    for f in range(fields):
        acc[...] = jnp.zeros_like(acc)
        found = number[f]

        def group(p, _):
            known, names, places = [], [], []
            for n in range(GROUP):
                known.append(GROUP * p + n < found)
                k = order[f * total + jnp.where(known[n], GROUP * p + n, 0)]
                count = jnp.where(known[n], live[k], 0)
                c = cells[pl.ds(k, 1), :]
                places.append(jnp.where(slot < count, c, -1))
                names.append(owner[k])
            at = [route_of(w % bands - band, bands) * sectors + w // bands for w in names]
            place = jnp.concatenate(places, axis=1)
            part = place // CELLS
            onehot = (site == jnp.where(place < 0, -1, place % CELLS)).astype(F32).astype(BF)
            j = jnp.concatenate([jacobian[w] for w in names], axis=1).astype(F32)
            columns = jnp.zeros_like(j)
            state = [outer[f, 0], *(inner[f, h] for h in range(parts - 2)), outer[f, 1]]
            found_all = jnp.dot(
                jnp.concatenate(state, axis=0), onehot, preferred_element_type=F32
            )
            for h in range(parts):
                columns = jnp.where(part == h, found_all[h * padded : (h + 1) * padded], columns)
            model = jnp.sum(j * columns, axis=0, keepdims=True)
            value, precision = j[levels : levels + 1], j[levels + 1 : levels + 2]
            res = precision * (model - value)
            for n in range(GROUP):

                @pl.when(known[n])
                def _():
                    route[pl.ds(at[n], 1), :] = res[:, n * LANES : (n + 1) * LANES]

            adjoint = j * res
            adjoint = jnp.concatenate(
                [jnp.where(part == h, adjoint, 0.0).astype(BF) for h in range(parts)], axis=0
            )
            acc[...] += lax.dot_general(adjoint, onehot, NT, preferred_element_type=F32)
            return 0

        lax.fori_loop(0, (found + GROUP - 1) // GROUP, group, 0)
        for h in range(parts):
            forcing = acc[pl.ds(h * padded, padded), :].astype(BF)
            out = lax.dot_general(forcing, vert[f], TN, preferred_element_type=F32)
            out = out[:, : 2 * LANES] + out[:, 2 * LANES :]
            at = pl.ds(h * CELLS, CELLS)
            lift[f, at, :] = out[:, :LANES]
            if f == 0:
                lift[fields, at, :] = out[:, LANES:]
            else:
                lift[fields, at, :] += out[:, LANES:]
        leaving += fetch([(lift.at[f], lift_far.at[f])], left.at[pl.ds(f, 1)])
    leaving += fetch([(lift.at[fields], lift_far.at[fields])], left.at[pl.ds(fields, 1)])

    for b in range(blocks):
        def line(j):
            return lift[b, pl.ds(j * LANES, LANES), :]

        for dst, first, second in (
            (low, tap_of(3, b, end) * line(end) + tap_of(4, b, end - 1) * line(end - 1),
             tap_of(4, b, end) * line(end)),
            (high, tap_of(0, b, 0) * line(0),
             tap_of(1, b, 0) * line(0) + tap_of(0, b, 1) * line(1)),
        ):
            dst[pl.ds(b * HALO * LANES, LANES), :] = first.astype(BF)
            dst[pl.ds((b * HALO + 1) * LANES, LANES), :] = second.astype(BF)
    for n, dst in ((1, low), (2, high)):
        both = jnp.concatenate(split(route[pl.ds(n * sectors, sectors), :]), axis=0)
        dst[pl.ds(blocks * HALO * LANES, 2 * sectors), :] = both
    leaving += fetch([(low, low_far), (high, high_far)], left.at[pl.ds(blocks, 2)])
    for n, dst in enumerate(residuals):
        source = 0 if n == 0 else n + 2
        dst[...] = route[pl.ds(source * sectors, sectors), :]
    for copy in leaving:
        copy.wait()


def respond_kernel(
    fields, rows, lift_far, taps_far, a_far, a_t, g_t, gq_t, gp_t, spread, lift, taps, pe_t, arrived
):
    blocks = fields + 1
    per = blocks * rows
    copies = fetch(
        [(a_far, a_t), (taps_far, taps)] + [(lift_far.at[b], lift.at[b]) for b in range(blocks)],
        arrived,
    )

    def east(i, p):
        at = step_rows(i, per)
        a = a_t[at, :]
        g_t[at, :] = jnp.sqrt((1.0 - a) * (1.0 + a))
        pe_t[at, :] = p
        return p * a

    def west(k, carry):
        w1, s = carry
        at = step_rows(LANES - 1 - k, per)
        a, g = a_t[at, :], g_t[at, :]
        t = w1 + g * pe_t[at, :]
        gq_t[at, :] = g * t
        gp_t[at, :] = g * s
        return a * t, a * s

    one = jnp.ones((per, LANES), F32)
    copies[0].wait()
    lax.fori_loop(0, LANES, east, one, unroll=4)
    lax.fori_loop(0, LANES, west, (jnp.zeros_like(one), one), unroll=4)
    copies[1].wait()
    for b in range(blocks):
        copies[2 + b].wait()
        for m in range(rows):
            total = taps[HALO, b, m : m + 1, :] * lift[b, pl.ds(m * LANES, LANES), :]
            for t in range(2 * HALO + 1):
                j = m - t + HALO
                if t != HALO and 0 <= j < rows:
                    total += taps[t, b, j : j + 1, :] * lift[b, pl.ds(j * LANES, LANES), :]
            spread[pl.ds(b * rows + m, LANES, stride=per), :] = total


def adjoint_kernel(fields, rows, spread, low, high, a_t, g_t, *rest):
    residuals = rest[:-4]
    u_t, ends, halo, pass_t = rest[-4:]
    blocks = fields + 1
    per = blocks * rows
    sectors = residuals[0].shape[0]
    riding = blocks * HALO * LANES
    parts = [residuals[0][...]]
    for src in (low, high):
        two = src[pl.ds(riding, 2 * sectors), :].astype(F32)
        parts.append(two[:sectors] + two[sectors:])
    parts += [a[...] for a in residuals[1:]]
    for n, part in enumerate(parts):
        ends[pl.ds(2 * per + n * sectors, sectors), :] = part

    for b in range(blocks):
        for n in range(HALO):
            at = pl.ds((b * HALO + n) * LANES, LANES)
            halo[pl.ds(b * rows + n, LANES, stride=per), :] = low[at, :].astype(F32)
            last = b * rows + rows - HALO + n
            halo[pl.ds(last, LANES, stride=per), :] = high[at, :].astype(F32)
    row = lax.broadcasted_iota(jnp.int32, (per, LANES), 0) % rows
    edge = (row < HALO) | (row >= rows - HALO)

    def east(i, q):
        at = step_rows(i, per)
        t = spread[at, :] + jnp.where(edge, halo[at, :], 0.0) + q
        pass_t[at, :] = g_t[at, :] * t
        return a_t[at, :] * t

    def west(k, p):
        at = step_rows(LANES - 1 - k, per)
        t = pass_t[at, :] + p
        u_t[at, :] = g_t[at, :] * t
        return a_t[at, :] * t

    zero = jnp.zeros((per, LANES), F32)
    ends[:per] = lax.fori_loop(0, LANES, east, zero, unroll=4)
    ends[per : 2 * per] = lax.fori_loop(0, LANES, west, zero, unroll=4)


def gradient_kernel(
    fields, levels, rows, count, bands, before, gathered, u_t, gq_t, gp_t, control,
    gradient, residual, full, extra, held, arrived,
):
    per = (fields + 1) * rows
    over, room = levels - LANES, LANES // fields
    me = lax.axis_index("lon")
    east_in, west_in = solve_sectors(
        me,
        [before[s, 0] for s in range(count)],
        [gathered[s, :per] for s in range(count)],
        [before[s, 3] for s in range(count)],
        [gathered[s, per : 2 * per] for s in range(count)],
    )
    for source in range(bands):
        route = route_of(lax.axis_index("lat") - source, bands)
        for s in range(count):
            line = gathered[s, pl.ds(2 * per + route * count + me, 1), :]
            residual[pl.ds(s * bands + source, 1), :] = line

    def one(i, _):
        at = step_rows(i, per)
        full[at, :] = u_t[at, :] + gq_t[at, :] * east_in + gp_t[at, :] * west_in
        return 0

    lax.fori_loop(0, LANES, one, 0, unroll=8)
    for j in range(rows):
        extra[j] = full[pl.ds(fields * rows + j, LANES, stride=per), :].T
    copies = []
    for f in range(fields):
        for j in range(rows):
            at = pl.ds(f * levels * rows + j, LANES, stride=rows)
            tile = full[pl.ds(f * rows + j, LANES, stride=per), :].T
            held[at, :] = control[at, :] + tile
            at = pl.ds((f * levels + LANES) * rows + j, over, stride=rows)
            held[at, :] = control[at, :] + extra[j, pl.ds(f * room, over), :]
        at = pl.ds(f * levels * rows, levels * rows)
        copies += fetch([(held.at[at], gradient.at[at])], arrived.at[pl.ds(f, 1)])
    for copy in copies:
        copy.wait()


def local(
    control, smoothing, lat_taps, vert_corr, obs_cell, obs_field, obs_count, obs_owner,
    obs_jacobian, obs_value, obs_precision,
):
    fields, levels, rows, longitudes = control.shape
    blocks = fields + 1
    per = blocks * rows
    count = lax.axis_size("lon")
    both = ("lon", "lat")
    total, slots = obs_cell.shape[1:]
    padded = -(-(levels + 2) // 16) * 16
    lines = longitudes * per
    line = sds((lines, LANES))

    sent = pl.pallas_call(
        functools.partial(pack_kernel, levels),
        out_shape=sds((total, padded, slots), BF),
        in_specs=[HBM] * 3,
        out_specs=HBM,
        scratch_shapes=[
            pltpu.VMEM((total // 16, levels, 16, slots), BF),
            pltpu.VMEM((2, total, slots), BF),
            pltpu.VMEM((padded * 16, slots), F32),
            pltpu.VMEM((total, padded, slots), BF),
            pltpu.SemaphoreType.DMA((2 + total // 16,)),
            pltpu.SemaphoreType.DMA((total // 16,)),
        ],
        compiler_params=params(FAR_MIB),
        cost_estimate=cost(3),
        name="pack",
    )(obs_jacobian[0], obs_value[0], obs_precision[0])
    jacobian = lax.all_to_all(sent, both, split_axis=0, concat_axis=0, tiled=True)

    vert_shape = (fields, padded, 4 * LANES)
    vert, taps = pl.pallas_call(
        functools.partial(prepare_kernel, fields, levels, rows),
        out_shape=[sds(vert_shape, BF), sds((2 * HALO + 1, blocks, rows, LANES))],
        in_specs=[VMEM] * 2,
        out_specs=[VMEM] * 2,
        scratch_shapes=[pltpu.VMEM((fields, padded, 2 * LANES), F32)],
        compiler_params=params(8),
        cost_estimate=cost(1),
        name="prepare",
    )(jnp.transpose(vert_corr, (1, 0, 2)), jnp.transpose(lat_taps, (1, 0, 2)))

    flat_control = control.reshape(fields * levels * rows, longitudes)
    flat_smoothing = smoothing.reshape(fields * levels * rows, longitudes)
    sizes = (fields, levels, rows)
    tiles = pltpu.VMEM((lines, LANES), F32)
    a_t, w0_t, w1_t, s_t, ends = pl.pallas_call(
        functools.partial(filter_kernel, *sizes),
        out_shape=[line] * 4 + [sds((4, per, LANES))],
        in_specs=[HBM] * 2,
        out_specs=[VMEM] * 5,
        scratch_shapes=[pltpu.VMEM(flat_control.shape, F32)] * 2
        + [tiles] * 4
        + [pltpu.VMEM((2, rows, LANES, LANES), F32), pltpu.SemaphoreType.DMA((2 * fields,))],
        compiler_params=params(34),
        cost_estimate=cost(6),
        name="filter_local",
    )(flat_control, flat_smoothing)
    gathered = lax.all_gather(ends, "lon")

    halo_rows = blocks * HALO * LANES
    halo_shape = sds((halo_rows, LANES), BF)
    low, high, entering = pl.pallas_call(
        functools.partial(edges_kernel, fields, rows, count),
        out_shape=[halo_shape, halo_shape, sds((2, per, LANES))],
        in_specs=[VMEM] * 4,
        out_specs=[VMEM] * 3,
        compiler_params=params(16),
        cost_estimate=cost(1),
        name="edges",
    )(gathered, w0_t, w1_t, s_t)

    bands = lax.axis_size("lat")
    up = [(i, i + 1) for i in range(bands - 1)]
    down = [(i + 1, i) for i in range(bands - 1)]
    after = lax.ppermute(low, "lat", down)
    before = lax.ppermute(high, "lat", up)
    sites = rows * longitudes
    inner_shape = (fields, sites // CELLS - 2, padded, CELLS)
    outer_shape = (fields, 2, padded, CELLS)
    partial_shape = (blocks, 2 * HALO, longitudes, LANES)
    inner, partial = pl.pallas_call(
        functools.partial(interior_kernel, fields, rows),
        out_shape=[sds(inner_shape, BF), sds(partial_shape)],
        in_specs=[VMEM] * 6,
        out_specs=[VMEM] * 2,
        scratch_shapes=[
            pltpu.VMEM((per, longitudes, LANES), F32),
            pltpu.VMEM((blocks, sites - 2 * CELLS, LANES), F32),
        ],
        compiler_params=params(16),
        cost_estimate=cost(3),
        name="interior",
    )(entering, w0_t, w1_t, s_t, taps, vert)

    outward = sds((halo_rows + 2 * count, LANES), BF)
    lift_shape = (blocks, sites, LANES)
    lift, low, high, *residuals = pl.pallas_call(
        functools.partial(observe_kernel, *sizes, bands),
        out_shape=[sds(lift_shape), outward, outward] + [sds((count, slots))] * (bands - 1),
        in_specs=[SMEM] * 3 + [VMEM] + [HBM] * 7,
        out_specs=[HBM] * 3 + [VMEM] * (bands - 1),
        scratch_shapes=[
            pltpu.VMEM(inner_shape, BF),
            pltpu.VMEM(partial_shape, F32),
            pltpu.VMEM(halo_shape.shape, BF),
            pltpu.VMEM(halo_shape.shape, BF),
            pltpu.VMEM(taps.shape, F32),
            pltpu.VMEM(vert.shape, BF),
            pltpu.VMEM(jacobian.shape, BF),
            pltpu.VMEM((blocks, 2 * CELLS, LANES), F32),
            pltpu.VMEM(outer_shape, BF),
            pltpu.VMEM(lift_shape, F32),
            pltpu.VMEM(outward.shape, BF),
            pltpu.VMEM(outward.shape, BF),
            pltpu.VMEM(((bands + 1) * count, slots), F32),
            pltpu.SMEM((fields * total,), jnp.int32),
            pltpu.SMEM((fields,), jnp.int32),
            pltpu.VMEM((sites // CELLS * padded, CELLS), F32),
            pltpu.SemaphoreType.DMA((7,)),
            pltpu.SemaphoreType.DMA((blocks + 2,)),
        ],
        compiler_params=params(FAR_MIB),
        cost_estimate=cost(14),
        name="observe",
    )(
        obs_field[0], obs_owner[0], obs_count[0], obs_cell[0],
        inner, partial, before, after, taps, vert, jacobian,
    )

    from_before = lax.ppermute(low, "lat", up)
    from_after = lax.ppermute(high, "lat", down)
    swap = [(0, bands - 1), (bands - 1, 0)]
    arrived = [residuals[0], lax.ppermute(residuals[1], "lat", swap)]
    for n in range(2, bands - 1):
        ring = [(i, (i + n) % bands) for i in range(bands)]
        arrived.append(lax.ppermute(residuals[n], "lat", ring))
    carried = 2 * per + (bands + 1) * count
    a_again, g_t, gq_t, gp_t, spread = pl.pallas_call(
        functools.partial(respond_kernel, fields, rows),
        out_shape=[line] * 5,
        in_specs=[HBM] * 3,
        out_specs=[VMEM] * 5,
        scratch_shapes=[
            pltpu.VMEM(lift_shape, F32),
            pltpu.VMEM(taps.shape, F32),
            tiles,
            pltpu.SemaphoreType.DMA((2 + blocks,)),
        ],
        compiler_params=params(36),
        cost_estimate=cost(5),
        name="respond",
    )(lift, taps, a_t)
    u_t, ends = pl.pallas_call(
        functools.partial(adjoint_kernel, fields, rows),
        out_shape=[line, sds((carried, LANES))],
        in_specs=[VMEM] * (5 + len(arrived)),
        out_specs=[VMEM] * 2,
        scratch_shapes=[tiles] * 2,
        compiler_params=params(20),
        cost_estimate=cost(3),
        name="adjoint_local",
    )(spread, from_before, from_after, a_again, g_t, *arrived)
    gathered_back = lax.all_gather(ends, "lon")
    gradient, returned = pl.pallas_call(
        functools.partial(gradient_kernel, *sizes, count, bands),
        out_shape=[sds(flat_control.shape), sds((total, slots))],
        in_specs=[VMEM] * 6,
        out_specs=[HBM, VMEM],
        scratch_shapes=[
            tiles,
            pltpu.VMEM((rows, LANES, LANES), F32),
            pltpu.VMEM(flat_control.shape, F32),
            pltpu.SemaphoreType.DMA((fields,)),
        ],
        compiler_params=params(20),
        cost_estimate=cost(3),
        name="gradient",
    )(gathered, gathered_back, u_t, gq_t, gp_t, flat_control)
    return gradient.reshape(control.shape), returned[None]


def solution(mesh):
    return jax.shard_map(
        local,
        mesh=mesh,
        in_specs=(
            P(None, None, "lat", "lon"),
            P(None, None, "lat", "lon"),
            P(None, None, "lat"),
            P(),
            P(("lon", "lat"), None, None),
            P(("lon", "lat"), None),
            P(("lon", "lat"), None),
            P(("lon", "lat"), None),
            P(("lon", "lat"), None, None, None),
            P(("lon", "lat"), None, None),
            P(("lon", "lat"), None, None),
        ),
        out_specs=(P(None, None, "lat", "lon"), P(("lon", "lat"), None, None)),
        check_vma=False,
    )
```

```python
import functools

import jax
import jax.numpy as jnp
from jax import lax
from jax.experimental import pallas as pl
from jax.experimental.pallas import tpu as pltpu
from jax.sharding import PartitionSpec as P

LANES = 128
HALO = 2
FAR_MIB = 60
ROOM = 12
CELLS = 256
GROUP = 4
BF = jnp.bfloat16
F32 = jnp.float32
NT = (((1,), (1,)), ((), ()))
TN = (((0,), (0,)), ((), ()))
VMEM = pl.BlockSpec(memory_space=pltpu.VMEM)
SMEM = pl.BlockSpec(memory_space=pltpu.SMEM)
HBM = pl.BlockSpec(memory_space=pltpu.HBM)


def params(mib):
    return pltpu.CompilerParams(vmem_limit_bytes=mib * 1024 * 1024)


def cost(microseconds):
    return pl.CostEstimate(
        flops=0, bytes_accessed=int(microseconds * 3.5e6), transcendentals=0
    )


def sds(shape, dtype=F32):
    return jax.ShapeDtypeStruct(shape, dtype)


def split(x):
    high = x.astype(BF)
    return high, (x - high.astype(F32)).astype(BF)


def step_rows(i, per):
    return pl.ds(pl.multiple_of(i * per, 8), per)


def solve_sectors(me, products, ends, cross, backs):
    count = len(products)
    whole, state = products[0], ends[0]
    for s in range(1, count):
        state = products[s] * state + ends[s]
        whole = whole * products[s]
    gap = 1.0 - whole
    east = state / gap
    east_in = jnp.zeros_like(east)
    turned = []
    for s in range(count):
        east_in = jnp.where(me == s, east, east_in)
        turned.append(backs[s] + cross[s] * east)
        east = products[s] * east + ends[s]
    state = turned[count - 1]
    for s in range(count - 2, -1, -1):
        state = products[s] * state + turned[s]
    west = state / gap
    west_in = jnp.zeros_like(west)
    for s in range(count - 1, -1, -1):
        west_in = jnp.where(me == s, west, west_in)
        west = products[s] * west + turned[s]
    return east_in, west_in


def fetch(pairs, arrived):
    copies = [pltpu.make_async_copy(a, b, arrived.at[n]) for n, (a, b) in enumerate(pairs)]
    for copy in copies:
        copy.start()
    return copies


def pack_kernel(levels, jacobian, value, precision, sent, held, small, wide, ready, arrived, left):
    blocks, padded = sent.shape[:2]
    chunk = held.shape[2]
    copies = fetch(
        [(value, small.at[0]), (precision, small.at[1])]
        + [
            (jacobian.at[:, pl.ds(c * chunk, chunk)], held.at[c])
            for c in range(blocks // chunk)
        ],
        arrived,
    )
    spare = (padded - levels - 2) * chunk
    wide[pl.ds((levels + 2) * chunk, spare), :] = jnp.zeros((spare, LANES), F32)
    copies[0].wait()
    copies[1].wait()
    leaving = []
    for c in range(blocks // chunk):
        copies[2 + c].wait()

        def put(l, _):
            wide[pl.ds(pl.multiple_of(l * chunk, 8), chunk), :] = held[c, l].astype(F32)
            return 0

        lax.fori_loop(0, levels, put, 0, unroll=8)
        for n in range(2):
            part = small[n, pl.ds(c * chunk, chunk), :].astype(F32)
            wide[pl.ds((levels + n) * chunk, chunk), :] = part
        for k in range(chunk):
            ready[c * chunk + k] = wide[pl.ds(k, padded, stride=chunk), :].astype(BF)
        at = pl.ds(c * chunk, chunk)
        leaving += fetch([(ready.at[at], sent.at[at])], left.at[pl.ds(c, 1)])
    for copy in leaving:
        copy.wait()


def prepare_kernel(fields, levels, rows, vert, lat_taps, both, taps, wide):
    over, room = levels - LANES, LANES // fields
    wide[...] = jnp.zeros_like(wide)
    for f in range(fields):
        v = vert[:, f, :]
        wide[f, :levels, :LANES] = v[:, :LANES]
        begin = LANES + f * room
        wide[f, :levels, begin : begin + over] = v[:, LANES:]
    both[:, :, : 2 * LANES], both[:, :, 2 * LANES :] = split(wide[...])
    diagonal = lax.broadcasted_iota(jnp.int32, (rows, rows), 0) == lax.broadcasted_iota(
        jnp.int32, (rows, rows), 1
    )
    lane = lax.broadcasted_iota(jnp.int32, (rows, LANES), 1) // room
    for t in range(2 * HALO + 1):
        last = jnp.zeros((rows, LANES), F32)
        for f in range(fields):
            line = jnp.broadcast_to(lat_taps[t, f : f + 1, :], (rows, rows))
            column = jnp.sum(jnp.where(diagonal, line, 0.0), axis=1, keepdims=True)
            column = jnp.broadcast_to(column, (rows, LANES))
            taps[t, f] = column
            last = jnp.where(lane == f, column, last)
        taps[t, fields] = last


def filter_kernel(
    fields, levels, rows, control, smoothing,
    a_far, w0_t, w1_t, s_t, ends,
    control_v, smoothing_v, a_t, g_t, x_t, e_t, pe_t, extra, arrived, left,
):
    per = (fields + 1) * rows
    over, room = levels - LANES, LANES // fields
    pairs = []
    for f in range(fields):
        at = pl.ds(f * levels * rows, levels * rows)
        pairs.append((smoothing.at[at], smoothing_v.at[at]))
        pairs.append((control.at[at], control_v.at[at]))
    copies = fetch(pairs, arrived)
    extra[...] = jnp.zeros_like(extra)
    for f in range(fields):
        for n, (src, dst) in enumerate(((smoothing_v, a_t), (control_v, x_t))):
            copies[2 * f + n].wait()
            for j in range(rows):
                tile = src[pl.ds(f * levels * rows + j, LANES, stride=rows), :]
                dst[pl.ds(f * rows + j, LANES, stride=per), :] = tile.T
                extra[n, j, pl.ds(f * room, over), :] = src[
                    pl.ds((f * levels + LANES) * rows + j, over, stride=rows), :
                ]
    for j in range(rows):
        at = pl.ds(fields * rows + j, LANES, stride=per)
        a_t[at, :] = extra[0, j].T
        x_t[at, :] = extra[1, j].T

    leaving = fetch([(a_t, a_far.at[pl.ds(0, a_t.shape[0])])], left)

    def east(i, carry):
        e, p = carry
        at = step_rows(i, per)
        a = a_t[at, :]
        g = jnp.sqrt((1.0 - a) * (1.0 + a))
        g_t[at, :] = g
        pe_t[at, :] = p
        e = a * e + g * x_t[at, :]
        e_t[at, :] = e
        return e, p * a

    zero = jnp.zeros((per, LANES), F32)
    one = jnp.ones((per, LANES), F32)
    e, p = lax.fori_loop(0, LANES, east, (zero, one), unroll=4)

    def west(k, carry):
        w0, w1, s = carry
        at = step_rows(LANES - 1 - k, per)
        a, g = a_t[at, :], g_t[at, :]
        w0 = a * w0 + g * e_t[at, :]
        w1 = a * (w1 + g * pe_t[at, :])
        s = a * s
        w0_t[at, :] = w0
        w1_t[at, :] = w1
        s_t[at, :] = s
        return w0, w1, s

    w0, w1, _ = lax.fori_loop(0, LANES, west, (zero, zero, one), unroll=4)
    ends[0] = p
    ends[1] = e
    ends[2] = w0
    ends[3] = w1
    for copy in leaving:
        copy.wait()


def put_halo(dst, b, fields, first, second):
    if b < fields:
        dst[pl.ds(b * HALO * LANES, LANES), :] = first.astype(BF)
        dst[pl.ds((b * HALO + 1) * LANES, LANES), :] = second.astype(BF)
    else:
        half = LANES // fields // 2
        both = first + pltpu.roll(second, half, 1)
        dst[pl.ds(b * HALO * LANES, LANES), :] = both.astype(BF)


def get_halo(src, b, fields):
    first = src[pl.ds(b * HALO * LANES, LANES), :].astype(F32)
    if b < fields:
        return first, src[pl.ds((b * HALO + 1) * LANES, LANES), :].astype(F32)
    return first, pltpu.roll(first, LANES - LANES // fields // 2, 1)


def edges_kernel(fields, rows, count, gathered, w0_t, w1_t, s_t, first, second, entering, sides):
    per = (fields + 1) * rows
    part = [[gathered[s, q] for s in range(count)] for q in range(4)]
    east_in, west_in = solve_sectors(lax.axis_index("lon"), part[0], part[1], part[3], part[2])
    entering[0] = east_in
    entering[1] = west_in
    odd = lax.axis_index("lat") % 2
    high, low = sides.at[odd], sides.at[1 - odd]
    for b in range(fields + 1):
        for begin, dst in ((b * rows, low), (b * rows + rows - HALO, high)):
            lines = []
            for n in range(begin, begin + HALO):
                at = pl.ds(n, LANES, stride=per)
                line = w0_t[at, :] + w1_t[at, :] * east_in[n : n + 1]
                lines.append(line + s_t[at, :] * west_in[n : n + 1])
            put_halo(dst, b, fields, *lines)
    first[...] = sides[0]
    second[...] = sides[1]


def vertical(vert, mixed):
    padded = vert.shape[0]
    v = jnp.concatenate([vert[:, : 2 * LANES], vert[:, 2 * LANES :]], axis=0)
    high, low = split(mixed)
    out = lax.dot_general(v, high, NT, preferred_element_type=F32)
    out = out[:padded] + out[padded:]
    out += lax.dot_general(v[:padded], low, NT, preferred_element_type=F32)
    return out.astype(BF)


def interior_kernel(fields, rows, entering, w0_t, w1_t, s_t, taps, vert, state, partial, western, mixed):
    blocks = fields + 1
    per = blocks * rows
    for n in range(per):
        at = pl.ds(n, LANES, stride=per)
        line = w0_t[at, :] + w1_t[at, :] * entering[0, n : n + 1, :]
        western[n] = line + s_t[at, :] * entering[1, n : n + 1, :]
    for b in range(blocks):
        for j in range(rows):
            total = taps[HALO, b, j : j + 1, :] * western[b * rows + j]
            for t in range(2 * HALO + 1):
                if t != HALO and 0 <= j + t - HALO < rows:
                    total += taps[t, b, j : j + 1, :] * western[b * rows + j + t - HALO]
            if HALO <= j < rows - HALO:
                mixed[b, pl.ds((j - HALO) * LANES, LANES), :] = total
            else:
                partial[b, j if j < HALO else j - rows + 2 * HALO] = total
    padded = vert.shape[1]
    for f in range(fields):
        for h in range(state.shape[1] // padded):
            at = pl.ds(h * CELLS, CELLS)
            both = jnp.concatenate([mixed[f, at, :], mixed[fields, at, :]], axis=1)
            state[f, pl.ds(h * padded, padded), :] = vertical(vert[f], both)


def route_of(delta, bands):
    cyclic = 2 + (delta + bands) % bands
    far = jnp.where(jnp.abs(delta) == bands - 1, 3, cyclic)
    near = jnp.where(delta == 1, 1, jnp.where(delta == -1, 2, 0))
    return jnp.where(jnp.abs(delta) <= 1, near, far)


def observe_kernel(
    fields, levels, rows, bands, field, owner, live, cells,
    inner_far, partial_far, first_far, second_far, taps_far, vert_far, jacobian_far, *rest,
):
    lift_far, first_out, second_out = rest[:3]
    residuals = rest[3 : 2 + bands]
    (
        state, partial, beside, taps, vert, jacobian, mixed, lift, sides,
        route, order, number, group_field, group_start, acc, arrived, left,
    ) = rest[2 + bands :]
    blocks = fields + 1
    band = lax.axis_index("lat")
    odd = band % 2
    after, before = beside.at[0], beside.at[1]
    low, high = sides.at[odd], sides.at[1 - odd]
    copies = fetch(
        [(first_far, beside.at[odd]), (second_far, beside.at[1 - odd])]
        + [(taps_far, taps), (partial_far, partial)]
        + [(vert_far, vert)],
        arrived,
    )
    total = field.shape[0]
    padded = vert.shape[1]
    parts = rows * LANES // CELLS
    wide = GROUP * LANES
    sectors = total // bands
    for f in range(fields):
        number[f] = 0

    def place(k, _):
        f = field[k]
        n = number[f]
        order[f * total + n] = k
        number[f] = n + 1
        return 0

    lax.fori_loop(0, total, place, 0)
    groups = 0
    for f in range(fields):
        here = (number[f] + GROUP - 1) // GROUP

        def put(p, _, f=f, first=groups):
            group_field[first + p] = f
            group_start[first + p] = GROUP * p
            return 0

        lax.fori_loop(0, here, put, 0)
        groups = groups + here
    acc[...] = jnp.zeros_like(acc)

    for n in range(4):
        copies[n].wait()
    copies += fetch(
        [(jacobian_far, jacobian)]
        + [
            (inner_far.at[f], state.at[f, pl.ds(padded, (parts - 2) * padded)])
            for f in range(fields)
        ],
        arrived.at[pl.ds(5, 1 + fields)],
    )

    def tap_of(t, b, j):
        return taps[t, b, j : j + 1, :]

    end = rows - 1
    for b in range(blocks):
        above, below = get_halo(before, b, fields), get_halo(after, b, fields)
        outer_rows = (
            partial[b, 0] + tap_of(0, b, 0) * above[0] + tap_of(1, b, 0) * above[1],
            partial[b, 1] + tap_of(0, b, 1) * above[1],
            partial[b, 2] + tap_of(4, b, end - 1) * below[0],
            partial[b, 3] + tap_of(3, b, end) * below[0] + tap_of(4, b, end) * below[1],
        )
        for n, line in enumerate(outer_rows):
            mixed[b, pl.ds(n * LANES, LANES), :] = line
    copies[4].wait()
    for f in range(fields):
        for h in range(2):
            at = pl.ds(h * CELLS, CELLS)
            both = jnp.concatenate([mixed[f, at, :], mixed[fields, at, :]], axis=1)
            state[f, pl.ds(h * (parts - 1) * padded, padded), :] = vertical(vert[f], both)

    for n in range(1 + fields):
        copies[5 + n].wait()
    site = lax.broadcasted_iota(jnp.int32, (CELLS, wide), 0)
    slot = lax.broadcasted_iota(jnp.int32, (1, LANES), 1)
    spare = (bands + 1) * sectors

    def group(p, _):
        f = group_field[p]
        places, names, at = [], [], []
        for n in range(GROUP):
            b = group_start[p] + n
            known = b < number[f]
            k = jnp.where(known, order[f * total + jnp.where(known, b, 0)], 0)
            count = jnp.where(known, live[k], 0)
            places.append(jnp.where(slot < count, cells[pl.ds(k, 1), :], -1))
            w = owner[k]
            names.append(w)
            to = route_of(w % bands - band, bands) * sectors + w // bands
            at.append(jnp.where(known, to, spare))
        place = jnp.concatenate(places, axis=1)
        part = place // CELLS
        onehot = (site == jnp.where(place < 0, -1, place % CELLS)).astype(F32).astype(BF)
        j = jnp.concatenate([jacobian[w] for w in names], axis=1).astype(F32)
        found_all = jnp.dot(state[f], onehot, preferred_element_type=F32)
        columns = jnp.zeros_like(j)
        for h in range(parts):
            columns = jnp.where(part == h, found_all[h * padded : (h + 1) * padded], columns)
        model = jnp.sum(j * columns, axis=0, keepdims=True)
        value, precision = j[levels : levels + 1], j[levels + 1 : levels + 2]
        res = precision * (model - value)
        adjoint = j * res
        adjoint = jnp.concatenate(
            [jnp.where(part == h, adjoint, 0.0).astype(BF) for h in range(parts)], axis=0
        )
        for n in range(GROUP):
            route[pl.ds(at[n], 1), :] = res[:, n * LANES : (n + 1) * LANES]
        acc[f] += lax.dot_general(adjoint, onehot, NT, preferred_element_type=F32)
        return 0

    lax.fori_loop(0, groups, group, 0)
    leaving = []
    for f in range(fields):
        for h in range(parts):
            forcing = acc[f, pl.ds(h * padded, padded), :].astype(BF)
            out = lax.dot_general(forcing, vert[f], TN, preferred_element_type=F32)
            out = out[:, : 2 * LANES] + out[:, 2 * LANES :]
            at = pl.ds(h * CELLS, CELLS)
            lift[f, at, :] = out[:, :LANES]
            if f == 0:
                lift[fields, at, :] = out[:, LANES:]
            else:
                lift[fields, at, :] += out[:, LANES:]
        leaving += fetch([(lift.at[f], lift_far.at[f])], left.at[pl.ds(f, 1)])
    leaving += fetch([(lift.at[fields], lift_far.at[fields])], left.at[pl.ds(fields, 1)])

    for b in range(blocks):
        def line(j):
            return lift[b, pl.ds(j * LANES, LANES), :]

        for dst, first, second in (
            (low, tap_of(3, b, end) * line(end) + tap_of(4, b, end - 1) * line(end - 1),
             tap_of(4, b, end) * line(end)),
            (high, tap_of(0, b, 0) * line(0),
             tap_of(1, b, 0) * line(0) + tap_of(0, b, 1) * line(1)),
        ):
            put_halo(dst, b, fields, first, second)
    riding = (fields * HALO + 1) * LANES
    for n, dst in ((1, low), (2, high)):
        both = jnp.concatenate(split(route[pl.ds(n * sectors, sectors), :]), axis=0)
        dst[pl.ds(riding, 2 * sectors), :] = both
    leaving += fetch(
        [(sides.at[0], first_out), (sides.at[1], second_out)], left.at[pl.ds(blocks, 2)]
    )
    for n, dst in enumerate(residuals):
        source = 0 if n == 0 else n + 2
        dst[...] = route[pl.ds(source * sectors, sectors), :]
    for copy in leaving:
        copy.wait()


def respond_kernel(
    fields, rows, lift_far, taps, a_far, a_t, g_t, gq_t, gp_t, spread, lift, pe_t, arrived
):
    blocks = fields + 1
    per = blocks * rows
    chunks = 4
    span = LANES // chunks
    parts = [pl.ds(c * span * per, span * per) for c in range(chunks)]
    copies = fetch([(a_far.at[at], a_t.at[at]) for at in parts], arrived)

    def east(i, p):
        at = step_rows(i, per)
        a = a_t[at, :]
        g_t[at, :] = jnp.sqrt((1.0 - a) * (1.0 + a))
        pe_t[at, :] = p
        return p * a

    def west(k, carry):
        w1, s = carry
        at = step_rows(LANES - 1 - k, per)
        a, g = a_t[at, :], g_t[at, :]
        t = w1 + g * pe_t[at, :]
        gq_t[at, :] = g * t
        gp_t[at, :] = g * s
        return a * t, a * s

    one = jnp.ones((per, LANES), F32)
    p = one
    for c, copy in enumerate(copies):
        copy.wait()
        if c == chunks // 2:
            copies_lift = fetch(
                [(lift_far.at[b], lift.at[b]) for b in range(blocks)],
                arrived.at[pl.ds(chunks, blocks)],
            )
        p = lax.fori_loop(c * span, (c + 1) * span, east, p, unroll=4)
    lax.fori_loop(0, LANES, west, (jnp.zeros_like(one), one), unroll=4)
    for b in range(blocks):
        copies_lift[b].wait()
        for m in range(rows):
            total = taps[HALO, b, m : m + 1, :] * lift[b, pl.ds(m * LANES, LANES), :]
            for t in range(2 * HALO + 1):
                j = m - t + HALO
                if t != HALO and 0 <= j < rows:
                    total += taps[t, b, j : j + 1, :] * lift[b, pl.ds(j * LANES, LANES), :]
            spread[pl.ds(b * rows + m, LANES, stride=per), :] = total


def adjoint_kernel(fields, rows, spread, first, second, a_t, g_t, *rest):
    residuals = rest[:-5]
    u_t, ends, halo, pass_t, beside = rest[-5:]
    odd = lax.axis_index("lat") % 2
    beside[odd] = first[...]
    beside[1 - odd] = second[...]
    high, low = beside.at[0], beside.at[1]
    blocks = fields + 1
    per = blocks * rows
    sectors = residuals[0].shape[0]
    riding = (fields * HALO + 1) * LANES
    parts = [residuals[0][...]]
    for src in (low, high):
        two = src[pl.ds(riding, 2 * sectors), :].astype(F32)
        parts.append(two[:sectors] + two[sectors:])
    parts += [a[...] for a in residuals[1:]]
    for n, part in enumerate(parts):
        ends[pl.ds(2 * per + n * sectors, sectors), :] = part

    for b in range(blocks):
        for src, begin in ((low, b * rows), (high, b * rows + rows - HALO)):
            for n, line in enumerate(get_halo(src, b, fields)):
                halo[pl.ds(begin + n, LANES, stride=per), :] = line
    row = lax.broadcasted_iota(jnp.int32, (per, LANES), 0) % rows
    edge = (row < HALO) | (row >= rows - HALO)

    def east(i, q):
        at = step_rows(i, per)
        t = spread[at, :] + jnp.where(edge, halo[at, :], 0.0) + q
        pass_t[at, :] = g_t[at, :] * t
        return a_t[at, :] * t

    def west(k, p):
        at = step_rows(LANES - 1 - k, per)
        t = pass_t[at, :] + p
        u_t[at, :] = g_t[at, :] * t
        return a_t[at, :] * t

    zero = jnp.zeros((per, LANES), F32)
    ends[:per] = lax.fori_loop(0, LANES, east, zero, unroll=4)
    ends[per : 2 * per] = lax.fori_loop(0, LANES, west, zero, unroll=4)


def gradient_kernel(
    fields, levels, rows, count, bands, before, gathered, u_t, gq_t, gp_t, control,
    gradient, residual, full, extra, held, arrived,
):
    per = (fields + 1) * rows
    over, room = levels - LANES, LANES // fields
    me = lax.axis_index("lon")
    east_in, west_in = solve_sectors(
        me,
        [before[s, 0] for s in range(count)],
        [gathered[s, :per] for s in range(count)],
        [before[s, 3] for s in range(count)],
        [gathered[s, per : 2 * per] for s in range(count)],
    )
    for source in range(bands):
        route = route_of(lax.axis_index("lat") - source, bands)
        for s in range(count):
            line = gathered[s, pl.ds(2 * per + route * count + me, 1), :]
            residual[pl.ds(s * bands + source, 1), :] = line

    def one(i, _):
        at = step_rows(i, per)
        full[at, :] = u_t[at, :] + gq_t[at, :] * east_in + gp_t[at, :] * west_in
        return 0

    lax.fori_loop(0, LANES, one, 0, unroll=8)
    for j in range(rows):
        extra[j] = full[pl.ds(fields * rows + j, LANES, stride=per), :].T
    copies = []
    for f in range(fields):
        for j in range(rows):
            at = pl.ds(f * levels * rows + j, LANES, stride=rows)
            tile = full[pl.ds(f * rows + j, LANES, stride=per), :].T
            held[at, :] = control[at, :] + tile
            at = pl.ds((f * levels + LANES) * rows + j, over, stride=rows)
            held[at, :] = control[at, :] + extra[j, pl.ds(f * room, over), :]
        at = pl.ds(f * levels * rows, levels * rows)
        copies += fetch([(held.at[at], gradient.at[at])], arrived.at[pl.ds(f, 1)])
    for copy in copies:
        copy.wait()


def local(
    control, smoothing, lat_taps, vert_corr, obs_cell, obs_field, obs_count, obs_owner,
    obs_jacobian, obs_value, obs_precision,
):
    fields, levels, rows, longitudes = control.shape
    blocks = fields + 1
    per = blocks * rows
    count = lax.axis_size("lon")
    both = ("lon", "lat")
    total, slots = obs_cell.shape[1:]
    padded = -(-(levels + 2) // 16) * 16
    lines = longitudes * per
    line = sds((lines, LANES))

    sent = pl.pallas_call(
        functools.partial(pack_kernel, levels),
        out_shape=sds((total, padded, slots), BF),
        in_specs=[HBM] * 3,
        out_specs=HBM,
        scratch_shapes=[
            pltpu.VMEM((total // 16, levels, 16, slots), BF),
            pltpu.VMEM((2, total, slots), BF),
            pltpu.VMEM((padded * 16, slots), F32),
            pltpu.VMEM((total, padded, slots), BF),
            pltpu.SemaphoreType.DMA((2 + total // 16,)),
            pltpu.SemaphoreType.DMA((total // 16,)),
        ],
        compiler_params=params(FAR_MIB),
        cost_estimate=cost(3),
        name="pack",
    )(obs_jacobian[0], obs_value[0], obs_precision[0])
    jacobian = lax.all_to_all(sent, both, split_axis=0, concat_axis=0, tiled=True)

    vert_shape = (fields, padded, 4 * LANES)
    vert, taps = pl.pallas_call(
        functools.partial(prepare_kernel, fields, levels, rows),
        out_shape=[sds(vert_shape, BF), sds((2 * HALO + 1, blocks, rows, LANES))],
        in_specs=[VMEM] * 2,
        out_specs=[VMEM] * 2,
        scratch_shapes=[pltpu.VMEM((fields, padded, 2 * LANES), F32)],
        compiler_params=params(8),
        cost_estimate=cost(1),
        name="prepare",
    )(jnp.transpose(vert_corr, (1, 0, 2)), jnp.transpose(lat_taps, (1, 0, 2)))

    flat_control = control.reshape(fields * levels * rows, longitudes)
    flat_smoothing = smoothing.reshape(fields * levels * rows, longitudes)
    sizes = (fields, levels, rows)
    tiles = pltpu.VMEM((lines, LANES), F32)
    a_far, w0_t, w1_t, s_t, ends = pl.pallas_call(
        functools.partial(filter_kernel, *sizes),
        out_shape=[sds((ROOM * lines, LANES))] + [line] * 3 + [sds((4, per, LANES))],
        in_specs=[HBM] * 2,
        out_specs=[HBM] + [VMEM] * 4,
        scratch_shapes=[pltpu.VMEM(flat_control.shape, F32)] * 2
        + [tiles] * 5
        + [
            pltpu.VMEM((2, rows, LANES, LANES), F32),
            pltpu.SemaphoreType.DMA((2 * fields,)),
            pltpu.SemaphoreType.DMA((1,)),
        ],
        compiler_params=params(34),
        cost_estimate=cost(6),
        name="filter_local",
    )(flat_control, flat_smoothing)
    gathered = lax.all_gather(ends, "lon")

    halo_rows = (fields * HALO + 1) * LANES
    halo_shape = sds((halo_rows, LANES), BF)
    first, second, entering = pl.pallas_call(
        functools.partial(edges_kernel, fields, rows, count),
        out_shape=[halo_shape, halo_shape, sds((2, per, LANES))],
        in_specs=[VMEM] * 4,
        out_specs=[VMEM] * 3,
        scratch_shapes=[pltpu.VMEM((2, *halo_shape.shape), BF)],
        compiler_params=params(16),
        cost_estimate=cost(1),
        name="edges",
    )(gathered, w0_t, w1_t, s_t)

    bands = lax.axis_size("lat")
    even = [p for i in range(0, bands - 1, 2) for p in ((i, i + 1), (i + 1, i))]
    odd = [p for i in range(1, bands - 1, 2) for p in ((i, i + 1), (i + 1, i))]
    first = lax.ppermute(first, "lat", even)
    second = lax.ppermute(second, "lat", odd)
    sites = rows * longitudes
    parts = sites // CELLS
    inner_shape = (fields, (parts - 2) * padded, CELLS)
    partial_shape = (blocks, 2 * HALO, longitudes, LANES)
    inner, partial = pl.pallas_call(
        functools.partial(interior_kernel, fields, rows),
        out_shape=[sds(inner_shape, BF), sds(partial_shape)],
        in_specs=[VMEM] * 6,
        out_specs=[VMEM] * 2,
        scratch_shapes=[
            pltpu.VMEM((per, longitudes, LANES), F32),
            pltpu.VMEM((blocks, sites - 2 * CELLS, LANES), F32),
        ],
        compiler_params=params(16),
        cost_estimate=cost(3),
        name="interior",
    )(entering, w0_t, w1_t, s_t, taps, vert)

    outward = sds((halo_rows + 2 * count, LANES), BF)
    lift_shape = (blocks, sites, LANES)
    lift, first, second, *residuals = pl.pallas_call(
        functools.partial(observe_kernel, *sizes, bands),
        out_shape=[sds((ROOM * blocks, sites, LANES)), outward, outward]
        + [sds((count, slots))] * (bands - 1),
        in_specs=[SMEM] * 3 + [VMEM] + [HBM] * 7,
        out_specs=[HBM] * 3 + [VMEM] * (bands - 1),
        scratch_shapes=[
            pltpu.VMEM((fields, parts * padded, CELLS), BF),
            pltpu.VMEM(partial_shape, F32),
            pltpu.VMEM((2, *halo_shape.shape), BF),
            pltpu.VMEM(taps.shape, F32),
            pltpu.VMEM(vert.shape, BF),
            pltpu.VMEM(jacobian.shape, BF),
            pltpu.VMEM((blocks, 2 * CELLS, LANES), F32),
            pltpu.VMEM(lift_shape, F32),
            pltpu.VMEM((2, *outward.shape), BF),
            pltpu.VMEM(((bands + 1) * count + 8, slots), F32),
            pltpu.SMEM((fields * total,), jnp.int32),
            pltpu.SMEM((fields,), jnp.int32),
            pltpu.SMEM((total // GROUP + fields,), jnp.int32),
            pltpu.SMEM((total // GROUP + fields,), jnp.int32),
            pltpu.VMEM((fields, parts * padded, CELLS), F32),
            pltpu.SemaphoreType.DMA((6 + fields,)),
            pltpu.SemaphoreType.DMA((blocks + 2,)),
        ],
        compiler_params=params(FAR_MIB),
        cost_estimate=cost(14),
        name="observe",
    )(
        obs_field[0], obs_owner[0], obs_count[0], obs_cell[0],
        inner, partial, first, second, taps, vert, jacobian,
    )

    swap = [(0, bands - 1), (bands - 1, 0)]
    arrived = [residuals[0], lax.ppermute(residuals[1], "lat", swap)]
    for n in range(2, bands - 1):
        ring = [(i, (i + n) % bands) for i in range(bands)]
        arrived.append(lax.ppermute(residuals[n], "lat", ring))
    first = lax.ppermute(first, "lat", even)
    second = lax.ppermute(second, "lat", odd)
    carried = 2 * per + (bands + 1) * count
    a_again, g_t, gq_t, gp_t, spread = pl.pallas_call(
        functools.partial(respond_kernel, fields, rows),
        out_shape=[line] * 5,
        in_specs=[HBM, VMEM, HBM],
        out_specs=[VMEM] * 5,
        scratch_shapes=[
            pltpu.VMEM(lift_shape, F32),
            tiles,
            pltpu.SemaphoreType.DMA((4 + blocks,)),
        ],
        compiler_params=params(36),
        cost_estimate=cost(5),
        name="respond",
    )(lift, taps, a_far)
    u_t, ends = pl.pallas_call(
        functools.partial(adjoint_kernel, fields, rows),
        out_shape=[line, sds((carried, LANES))],
        in_specs=[VMEM] * (5 + len(arrived)),
        out_specs=[VMEM] * 2,
        scratch_shapes=[tiles] * 2 + [pltpu.VMEM((2, *outward.shape), BF)],
        compiler_params=params(20),
        cost_estimate=cost(3),
        name="adjoint_local",
    )(spread, first, second, a_again, g_t, *arrived)
    gathered_back = lax.all_gather(ends, "lon")
    gradient, returned = pl.pallas_call(
        functools.partial(gradient_kernel, *sizes, count, bands),
        out_shape=[sds(flat_control.shape), sds((total, slots))],
        in_specs=[VMEM] * 6,
        out_specs=[HBM, VMEM],
        scratch_shapes=[
            tiles,
            pltpu.VMEM((rows, LANES, LANES), F32),
            pltpu.VMEM(flat_control.shape, F32),
            pltpu.SemaphoreType.DMA((fields,)),
        ],
        compiler_params=params(20),
        cost_estimate=cost(3),
        name="gradient",
    )(gathered, gathered_back, u_t, gq_t, gp_t, flat_control)
    return gradient.reshape(control.shape), returned[None]


def solution(mesh):
    return jax.shard_map(
        local,
        mesh=mesh,
        in_specs=(
            P(None, None, "lat", "lon"),
            P(None, None, "lat", "lon"),
            P(None, None, "lat"),
            P(),
            P(("lon", "lat"), None, None),
            P(("lon", "lat"), None),
            P(("lon", "lat"), None),
            P(("lon", "lat"), None),
            P(("lon", "lat"), None, None, None),
            P(("lon", "lat"), None, None),
            P(("lon", "lat"), None, None),
        ),
        out_specs=(P(None, None, "lat", "lon"), P(("lon", "lat"), None, None)),
        check_vma=False,
    )
```

```python
import functools

import jax
import jax.numpy as jnp
from jax import lax
from jax.experimental import pallas as pl
from jax.experimental.pallas import tpu as pltpu
from jax.sharding import PartitionSpec as P

LANES = 128
HALO = 2
OBS_MIB = 28
FAR_MIB = 60
ROOM = 12
FAR = 24
CELLS = 256
GROUP = 4
BF = jnp.bfloat16
F32 = jnp.float32
NT = (((1,), (1,)), ((), ()))
TN = (((0,), (0,)), ((), ()))
VMEM = pl.BlockSpec(memory_space=pltpu.VMEM)
SMEM = pl.BlockSpec(memory_space=pltpu.SMEM)
HBM = pl.BlockSpec(memory_space=pltpu.HBM)


def params(mib):
    return pltpu.CompilerParams(vmem_limit_bytes=mib * 1024 * 1024)


def cost(microseconds):
    return pl.CostEstimate(
        flops=0, bytes_accessed=int(microseconds * 3.5e6), transcendentals=0
    )


def sds(shape, dtype=F32):
    return jax.ShapeDtypeStruct(shape, dtype)


def split(x):
    high = x.astype(BF)
    return high, (x - high.astype(F32)).astype(BF)


def step_rows(i, per):
    return pl.ds(pl.multiple_of(i * per, 8), per)


def solve_sectors(me, products, ends, cross, backs):
    count = len(products)
    whole, state = products[0], ends[0]
    for s in range(1, count):
        state = products[s] * state + ends[s]
        whole = whole * products[s]
    gap = 1.0 - whole
    east = state / gap
    east_in = jnp.zeros_like(east)
    turned = []
    for s in range(count):
        east_in = jnp.where(me == s, east, east_in)
        turned.append(backs[s] + cross[s] * east)
        east = products[s] * east + ends[s]
    state = turned[count - 1]
    for s in range(count - 2, -1, -1):
        state = products[s] * state + turned[s]
    west = state / gap
    west_in = jnp.zeros_like(west)
    for s in range(count - 1, -1, -1):
        west_in = jnp.where(me == s, west, west_in)
        west = products[s] * west + turned[s]
    return east_in, west_in


def fetch(pairs, arrived):
    copies = [pltpu.make_async_copy(a, b, arrived.at[n]) for n, (a, b) in enumerate(pairs)]
    for copy in copies:
        copy.start()
    return copies


def pack_kernel(levels, jacobian, value, precision, sent, held, small, wide, ready, arrived, left):
    blocks, padded = sent.shape[:2]
    chunk = held.shape[2]
    copies = fetch(
        [(value, small.at[0]), (precision, small.at[1])]
        + [
            (jacobian.at[:, pl.ds(c * chunk, chunk)], held.at[c])
            for c in range(blocks // chunk)
        ],
        arrived,
    )
    spare = (padded - levels - 2) * chunk
    wide[pl.ds((levels + 2) * chunk, spare), :] = jnp.zeros((spare, LANES), F32)
    copies[0].wait()
    copies[1].wait()
    leaving = []
    for c in range(blocks // chunk):
        copies[2 + c].wait()

        def put(l, _):
            wide[pl.ds(pl.multiple_of(l * chunk, 8), chunk), :] = held[c, l].astype(F32)
            return 0

        lax.fori_loop(0, levels, put, 0, unroll=8)
        for n in range(2):
            part = small[n, pl.ds(c * chunk, chunk), :].astype(F32)
            wide[pl.ds((levels + n) * chunk, chunk), :] = part
        for k in range(chunk):
            ready[c * chunk + k] = wide[pl.ds(k, padded, stride=chunk), :].astype(BF)
        at = pl.ds(c * chunk, chunk)
        leaving += fetch([(ready.at[at], sent.at[at])], left.at[pl.ds(c, 1)])
    for copy in leaving:
        copy.wait()


def prepare_kernel(fields, levels, rows, vert, lat_taps, both, taps, wide):
    over, room = levels - LANES, LANES // fields
    wide[...] = jnp.zeros_like(wide)
    for f in range(fields):
        v = vert[:, f, :]
        wide[f, :levels, :LANES] = v[:, :LANES]
        begin = LANES + f * room
        wide[f, :levels, begin : begin + over] = v[:, LANES:]
    both[:, :, : 2 * LANES], both[:, :, 2 * LANES :] = split(wide[...])
    diagonal = lax.broadcasted_iota(jnp.int32, (rows, rows), 0) == lax.broadcasted_iota(
        jnp.int32, (rows, rows), 1
    )
    lane = lax.broadcasted_iota(jnp.int32, (rows, LANES), 1) // room
    for t in range(2 * HALO + 1):
        last = jnp.zeros((rows, LANES), F32)
        for f in range(fields):
            line = jnp.broadcast_to(lat_taps[t, f : f + 1, :], (rows, rows))
            column = jnp.sum(jnp.where(diagonal, line, 0.0), axis=1, keepdims=True)
            column = jnp.broadcast_to(column, (rows, LANES))
            taps[t, f] = column
            last = jnp.where(lane == f, column, last)
        taps[t, fields] = last


def filter_kernel(
    fields, levels, rows, control, smoothing,
    a_far, w0_t, w1_t, s_t, ends,
    control_v, smoothing_v, a_t, g_t, x_t, e_t, pe_t, extra, arrived, left,
):
    per = (fields + 1) * rows
    over, room = levels - LANES, LANES // fields
    pairs = []
    for f in range(fields):
        at = pl.ds(f * levels * rows, levels * rows)
        pairs.append((smoothing.at[at], smoothing_v.at[at]))
        pairs.append((control.at[at], control_v.at[at]))
    copies = fetch(pairs, arrived)
    extra[...] = jnp.zeros_like(extra)
    for f in range(fields):
        for n, (src, dst) in enumerate(((smoothing_v, a_t), (control_v, x_t))):
            copies[2 * f + n].wait()
            for j in range(rows):
                tile = src[pl.ds(f * levels * rows + j, LANES, stride=rows), :]
                dst[pl.ds(f * rows + j, LANES, stride=per), :] = tile.T
                extra[n, j, pl.ds(f * room, over), :] = src[
                    pl.ds((f * levels + LANES) * rows + j, over, stride=rows), :
                ]
    for j in range(rows):
        at = pl.ds(fields * rows + j, LANES, stride=per)
        a_t[at, :] = extra[0, j].T
        x_t[at, :] = extra[1, j].T

    leaving = fetch([(a_t, a_far.at[pl.ds(0, a_t.shape[0])])], left)

    def east(i, carry):
        e, p = carry
        at = step_rows(i, per)
        a = a_t[at, :]
        g = jnp.sqrt((1.0 - a) * (1.0 + a))
        g_t[at, :] = g
        pe_t[at, :] = p
        e = a * e + g * x_t[at, :]
        e_t[at, :] = e
        return e, p * a

    zero = jnp.zeros((per, LANES), F32)
    one = jnp.ones((per, LANES), F32)
    e, p = lax.fori_loop(0, LANES, east, (zero, one), unroll=4)

    def west(k, carry):
        w0, w1, s = carry
        at = step_rows(LANES - 1 - k, per)
        a, g = a_t[at, :], g_t[at, :]
        w0 = a * w0 + g * e_t[at, :]
        w1 = a * (w1 + g * pe_t[at, :])
        s = a * s
        w0_t[at, :] = w0
        w1_t[at, :] = w1
        s_t[at, :] = s
        return w0, w1, s

    w0, w1, _ = lax.fori_loop(0, LANES, west, (zero, zero, one), unroll=4)
    ends[0] = p
    ends[1] = e
    ends[2] = w0
    ends[3] = w1
    for copy in leaving:
        copy.wait()


def put_halo(dst, b, fields, first, second):
    if b < fields:
        dst[pl.ds(b * HALO * LANES, LANES), :] = first.astype(BF)
        dst[pl.ds((b * HALO + 1) * LANES, LANES), :] = second.astype(BF)
    else:
        half = LANES // fields // 2
        both = first + pltpu.roll(second, half, 1)
        dst[pl.ds(b * HALO * LANES, LANES), :] = both.astype(BF)


def get_halo(src, b, fields):
    first = src[pl.ds(b * HALO * LANES, LANES), :].astype(F32)
    if b < fields:
        return first, src[pl.ds((b * HALO + 1) * LANES, LANES), :].astype(F32)
    return first, pltpu.roll(first, LANES - LANES // fields // 2, 1)


def edges_kernel(fields, rows, count, gathered, w0_t, w1_t, s_t, first, second, entering, sides):
    per = (fields + 1) * rows
    part = [[gathered[s, q] for s in range(count)] for q in range(4)]
    east_in, west_in = solve_sectors(lax.axis_index("lon"), part[0], part[1], part[3], part[2])
    entering[0] = east_in
    entering[1] = west_in
    odd = lax.axis_index("lat") % 2
    high, low = sides.at[odd], sides.at[1 - odd]
    for b in range(fields + 1):
        for begin, dst in ((b * rows, low), (b * rows + rows - HALO, high)):
            lines = []
            for n in range(begin, begin + HALO):
                at = pl.ds(n, LANES, stride=per)
                line = w0_t[at, :] + w1_t[at, :] * east_in[n : n + 1]
                lines.append(line + s_t[at, :] * west_in[n : n + 1])
            put_halo(dst, b, fields, *lines)
    first[...] = sides[0]
    second[...] = sides[1]


def vertical(vert, mixed):
    padded = vert.shape[0]
    v = jnp.concatenate([vert[:, : 2 * LANES], vert[:, 2 * LANES :]], axis=0)
    high, low = split(mixed)
    out = lax.dot_general(v, high, NT, preferred_element_type=F32)
    out = out[:padded] + out[padded:]
    out += lax.dot_general(v[:padded], low, NT, preferred_element_type=F32)
    return out.astype(BF)


def interior_kernel(
    fields, rows, entering, w0_t, w1_t, s_t, taps, vert, state_far, partial_far,
    state, partial, western, mixed, left,
):
    blocks = fields + 1
    per = blocks * rows
    for n in range(per):
        at = pl.ds(n, LANES, stride=per)
        line = w0_t[at, :] + w1_t[at, :] * entering[0, n : n + 1, :]
        western[n] = line + s_t[at, :] * entering[1, n : n + 1, :]
    for b in range(blocks):
        for j in range(rows):
            total = taps[HALO, b, j : j + 1, :] * western[b * rows + j]
            for t in range(2 * HALO + 1):
                if t != HALO and 0 <= j + t - HALO < rows:
                    total += taps[t, b, j : j + 1, :] * western[b * rows + j + t - HALO]
            if HALO <= j < rows - HALO:
                mixed[b, pl.ds((j - HALO) * LANES, LANES), :] = total
            else:
                partial[b, j if j < HALO else j - rows + 2 * HALO] = total
    padded = vert.shape[1]
    leaving = fetch([(partial, partial_far.at[pl.ds(0, blocks)])], left.at[pl.ds(fields, 1)])
    for f in range(fields):
        for h in range(state.shape[1] // padded):
            at = pl.ds(h * CELLS, CELLS)
            both = jnp.concatenate([mixed[f, at, :], mixed[fields, at, :]], axis=1)
            state[f, pl.ds(h * padded, padded), :] = vertical(vert[f], both)
        leaving += fetch([(state.at[f], state_far.at[f])], left.at[pl.ds(f, 1)])
    for copy in leaving:
        copy.wait()


def stage_kernel(
    fields, levels, rows, inner_far, partial_far, jacobian_far, vert_corr, lat_taps,
    inner, partial, jacobian, vert, taps, wide, arrived,
):
    copies = fetch(
        [
            (jacobian_far, jacobian),
            (partial_far.at[pl.ds(0, fields + 1)], partial),
            (inner_far.at[pl.ds(0, fields)], inner),
        ],
        arrived,
    )
    prepare_kernel(fields, levels, rows, vert_corr, lat_taps, vert, taps, wide)
    for copy in copies:
        copy.wait()


def route_of(delta, bands):
    cyclic = 2 + (delta + bands) % bands
    far = jnp.where(jnp.abs(delta) == bands - 1, 3, cyclic)
    near = jnp.where(delta == 1, 1, jnp.where(delta == -1, 2, 0))
    return jnp.where(jnp.abs(delta) <= 1, near, far)


def observe_kernel(
    fields, levels, rows, bands, field, owner, live, cells,
    inner, partial, first_far, second_far, taps, vert, jacobian, *rest,
):
    lift, first_out, second_out = rest[:3]
    residuals = rest[3 : 2 + bands]
    (
        state, beside, mixed, sides,
        route, order, number, group_field, group_start, acc, arrived,
    ) = rest[2 + bands :]
    blocks = fields + 1
    band = lax.axis_index("lat")
    odd = band % 2
    after, before = beside.at[0], beside.at[1]
    low, high = sides.at[odd], sides.at[1 - odd]
    copies = fetch([(first_far, beside.at[odd]), (second_far, beside.at[1 - odd])], arrived)
    total = field.shape[0]
    padded = vert.shape[1]
    parts = rows * LANES // CELLS
    wide = GROUP * LANES
    sectors = total // bands
    for f in range(fields):
        number[f] = 0

    def place(k, _):
        f = field[k]
        n = number[f]
        order[f * total + n] = k
        number[f] = n + 1
        return 0

    lax.fori_loop(0, total, place, 0)
    groups = 0
    for f in range(fields):
        here = (number[f] + GROUP - 1) // GROUP

        def put(p, _, f=f, first=groups):
            group_field[first + p] = f
            group_start[first + p] = GROUP * p
            return 0

        lax.fori_loop(0, here, put, 0)
        groups = groups + here
    acc[...] = jnp.zeros_like(acc)

    for f in range(fields):
        state[f, pl.ds(padded, (parts - 2) * padded), :] = inner[f]
    for copy in copies:
        copy.wait()

    def tap_of(t, b, j):
        return taps[t, b, j : j + 1, :]

    end = rows - 1
    for b in range(blocks):
        above, below = get_halo(before, b, fields), get_halo(after, b, fields)
        outer_rows = (
            partial[b, 0] + tap_of(0, b, 0) * above[0] + tap_of(1, b, 0) * above[1],
            partial[b, 1] + tap_of(0, b, 1) * above[1],
            partial[b, 2] + tap_of(4, b, end - 1) * below[0],
            partial[b, 3] + tap_of(3, b, end) * below[0] + tap_of(4, b, end) * below[1],
        )
        for n, line in enumerate(outer_rows):
            mixed[b, pl.ds(n * LANES, LANES), :] = line
    for f in range(fields):
        for h in range(2):
            at = pl.ds(h * CELLS, CELLS)
            both = jnp.concatenate([mixed[f, at, :], mixed[fields, at, :]], axis=1)
            state[f, pl.ds(h * (parts - 1) * padded, padded), :] = vertical(vert[f], both)

    site = lax.broadcasted_iota(jnp.int32, (CELLS, wide), 0)
    slot = lax.broadcasted_iota(jnp.int32, (1, LANES), 1)
    spare = (bands + 1) * sectors

    def group(p, _):
        f = group_field[p]
        places, names, at = [], [], []
        for n in range(GROUP):
            b = group_start[p] + n
            known = b < number[f]
            k = jnp.where(known, order[f * total + jnp.where(known, b, 0)], 0)
            count = jnp.where(known, live[k], 0)
            places.append(jnp.where(slot < count, cells[pl.ds(k, 1), :], -1))
            w = owner[k]
            names.append(w)
            to = route_of(w % bands - band, bands) * sectors + w // bands
            at.append(jnp.where(known, to, spare))
        place = jnp.concatenate(places, axis=1)
        part = place // CELLS
        onehot = (site == jnp.where(place < 0, -1, place % CELLS)).astype(F32).astype(BF)
        j = jnp.concatenate([jacobian[w] for w in names], axis=1).astype(F32)
        found_all = jnp.dot(state[f], onehot, preferred_element_type=F32)
        columns = jnp.zeros_like(j)
        for h in range(parts):
            columns = jnp.where(part == h, found_all[h * padded : (h + 1) * padded], columns)
        model = jnp.sum(j * columns, axis=0, keepdims=True)
        value, precision = j[levels : levels + 1], j[levels + 1 : levels + 2]
        res = precision * (model - value)
        adjoint = (j * res).astype(BF)
        adjoint = jnp.concatenate(
            [adjoint * (part == h).astype(F32).astype(BF) for h in range(parts)], axis=0
        )
        for n in range(GROUP):
            route[pl.ds(at[n], 1), :] = res[:, n * LANES : (n + 1) * LANES]
        acc[f] += lax.dot_general(adjoint, onehot, NT, preferred_element_type=F32)
        return 0

    lax.fori_loop(0, groups, group, 0)
    for f in range(fields):
        for h in range(parts):
            forcing = acc[f, pl.ds(h * padded, padded), :].astype(BF)
            out = lax.dot_general(forcing, vert[f], TN, preferred_element_type=F32)
            out = out[:, : 2 * LANES] + out[:, 2 * LANES :]
            at = pl.ds(h * CELLS, CELLS)
            lift[f, at, :] = out[:, :LANES]
            if f == 0:
                lift[fields, at, :] = out[:, LANES:]
            else:
                lift[fields, at, :] += out[:, LANES:]

    for b in range(blocks):
        def line(j):
            return lift[b, pl.ds(j * LANES, LANES), :]

        for dst, first, second in (
            (low, tap_of(3, b, end) * line(end) + tap_of(4, b, end - 1) * line(end - 1),
             tap_of(4, b, end) * line(end)),
            (high, tap_of(0, b, 0) * line(0),
             tap_of(1, b, 0) * line(0) + tap_of(0, b, 1) * line(1)),
        ):
            put_halo(dst, b, fields, first, second)
    riding = (fields * HALO + 1) * LANES
    for n, dst in ((1, low), (2, high)):
        both = jnp.concatenate(split(route[pl.ds(n * sectors, sectors), :]), axis=0)
        dst[pl.ds(riding, 2 * sectors), :] = both
    first_out[...] = sides[0]
    second_out[...] = sides[1]
    for n, dst in enumerate(residuals):
        source = 0 if n == 0 else n + 2
        dst[...] = route[pl.ds(source * sectors, sectors), :]


def respond_kernel(
    fields, rows, lift, taps, a_far, a_t, g_t, gq_t, gp_t, spread, pe_t, arrived
):
    blocks = fields + 1
    per = blocks * rows
    chunks = 4
    span = LANES // chunks
    parts = [pl.ds(c * span * per, span * per) for c in range(chunks)]
    copies = fetch([(a_far.at[at], a_t.at[at]) for at in parts], arrived)

    def east(i, p):
        at = step_rows(i, per)
        a = a_t[at, :]
        g_t[at, :] = jnp.sqrt((1.0 - a) * (1.0 + a))
        pe_t[at, :] = p
        return p * a

    def west(k, carry):
        w1, s = carry
        at = step_rows(LANES - 1 - k, per)
        a, g = a_t[at, :], g_t[at, :]
        t = w1 + g * pe_t[at, :]
        gq_t[at, :] = g * t
        gp_t[at, :] = g * s
        return a * t, a * s

    one = jnp.ones((per, LANES), F32)
    p = one
    for c, copy in enumerate(copies):
        copy.wait()
        p = lax.fori_loop(c * span, (c + 1) * span, east, p, unroll=4)
    lax.fori_loop(0, LANES, west, (jnp.zeros_like(one), one), unroll=4)
    for b in range(blocks):
        for m in range(rows):
            total = taps[HALO, b, m : m + 1, :] * lift[b, pl.ds(m * LANES, LANES), :]
            for t in range(2 * HALO + 1):
                j = m - t + HALO
                if t != HALO and 0 <= j < rows:
                    total += taps[t, b, j : j + 1, :] * lift[b, pl.ds(j * LANES, LANES), :]
            spread[pl.ds(b * rows + m, LANES, stride=per), :] = total


def adjoint_kernel(fields, rows, spread, first, second, a_t, g_t, *rest):
    residuals = rest[:-5]
    u_t, ends, halo, pass_t, beside = rest[-5:]
    odd = lax.axis_index("lat") % 2
    beside[odd] = first[...]
    beside[1 - odd] = second[...]
    high, low = beside.at[0], beside.at[1]
    blocks = fields + 1
    per = blocks * rows
    sectors = residuals[0].shape[0]
    riding = (fields * HALO + 1) * LANES
    parts = [residuals[0][...]]
    for src in (low, high):
        two = src[pl.ds(riding, 2 * sectors), :].astype(F32)
        parts.append(two[:sectors] + two[sectors:])
    parts += [a[...] for a in residuals[1:]]
    for n, part in enumerate(parts):
        ends[pl.ds(2 * per + n * sectors, sectors), :] = part

    for b in range(blocks):
        for src, begin in ((low, b * rows), (high, b * rows + rows - HALO)):
            for n, line in enumerate(get_halo(src, b, fields)):
                halo[pl.ds(begin + n, LANES, stride=per), :] = line
    row = lax.broadcasted_iota(jnp.int32, (per, LANES), 0) % rows
    edge = (row < HALO) | (row >= rows - HALO)

    def east(i, q):
        at = step_rows(i, per)
        t = spread[at, :] + jnp.where(edge, halo[at, :], 0.0) + q
        pass_t[at, :] = g_t[at, :] * t
        return a_t[at, :] * t

    def west(k, p):
        at = step_rows(LANES - 1 - k, per)
        t = pass_t[at, :] + p
        u_t[at, :] = g_t[at, :] * t
        return a_t[at, :] * t

    zero = jnp.zeros((per, LANES), F32)
    ends[:per] = lax.fori_loop(0, LANES, east, zero, unroll=4)
    ends[per : 2 * per] = lax.fori_loop(0, LANES, west, zero, unroll=4)


def gradient_kernel(
    fields, levels, rows, count, bands, before, gathered, u_t, gq_t, gp_t, control,
    gradient, residual, full, extra, held, arrived,
):
    per = (fields + 1) * rows
    over, room = levels - LANES, LANES // fields
    me = lax.axis_index("lon")
    east_in, west_in = solve_sectors(
        me,
        [before[s, 0] for s in range(count)],
        [gathered[s, :per] for s in range(count)],
        [before[s, 3] for s in range(count)],
        [gathered[s, per : 2 * per] for s in range(count)],
    )
    for source in range(bands):
        route = route_of(lax.axis_index("lat") - source, bands)
        for s in range(count):
            line = gathered[s, pl.ds(2 * per + route * count + me, 1), :]
            residual[pl.ds(s * bands + source, 1), :] = line

    def one(i, _):
        at = step_rows(i, per)
        full[at, :] = u_t[at, :] + gq_t[at, :] * east_in + gp_t[at, :] * west_in
        return 0

    lax.fori_loop(0, LANES, one, 0, unroll=8)
    for j in range(rows):
        extra[j] = full[pl.ds(fields * rows + j, LANES, stride=per), :].T
    copies = []
    for f in range(fields):
        for j in range(rows):
            at = pl.ds(f * levels * rows + j, LANES, stride=rows)
            tile = full[pl.ds(f * rows + j, LANES, stride=per), :].T
            held[at, :] = control[at, :] + tile
            at = pl.ds((f * levels + LANES) * rows + j, over, stride=rows)
            held[at, :] = control[at, :] + extra[j, pl.ds(f * room, over), :]
        at = pl.ds(f * levels * rows, levels * rows)
        copies += fetch([(held.at[at], gradient.at[at])], arrived.at[pl.ds(f, 1)])
    for copy in copies:
        copy.wait()


def local(
    control, smoothing, lat_taps, vert_corr, obs_cell, obs_field, obs_count, obs_owner,
    obs_jacobian, obs_value, obs_precision,
):
    fields, levels, rows, longitudes = control.shape
    blocks = fields + 1
    per = blocks * rows
    count = lax.axis_size("lon")
    both = ("lon", "lat")
    total, slots = obs_cell.shape[1:]
    padded = -(-(levels + 2) // 16) * 16
    lines = longitudes * per
    line = sds((lines, LANES))

    sent = pl.pallas_call(
        functools.partial(pack_kernel, levels),
        out_shape=sds((total, padded, slots), BF),
        in_specs=[HBM] * 3,
        out_specs=HBM,
        scratch_shapes=[
            pltpu.VMEM((total // 16, levels, 16, slots), BF),
            pltpu.VMEM((2, total, slots), BF),
            pltpu.VMEM((padded * 16, slots), F32),
            pltpu.VMEM((total, padded, slots), BF),
            pltpu.SemaphoreType.DMA((2 + total // 16,)),
            pltpu.SemaphoreType.DMA((total // 16,)),
        ],
        compiler_params=params(FAR_MIB),
        cost_estimate=cost(3),
        name="pack",
    )(obs_jacobian[0], obs_value[0], obs_precision[0])
    jacobian = lax.all_to_all(sent, both, split_axis=0, concat_axis=0, tiled=True)

    vert_shape = (fields, padded, 4 * LANES)
    vert, taps = pl.pallas_call(
        functools.partial(prepare_kernel, fields, levels, rows),
        out_shape=[sds(vert_shape, BF), sds((2 * HALO + 1, blocks, rows, LANES))],
        in_specs=[VMEM] * 2,
        out_specs=[VMEM] * 2,
        scratch_shapes=[pltpu.VMEM((fields, padded, 2 * LANES), F32)],
        compiler_params=params(8),
        cost_estimate=cost(1),
        name="prepare",
    )(jnp.transpose(vert_corr, (1, 0, 2)), jnp.transpose(lat_taps, (1, 0, 2)))

    flat_control = control.reshape(fields * levels * rows, longitudes)
    flat_smoothing = smoothing.reshape(fields * levels * rows, longitudes)
    sizes = (fields, levels, rows)
    tiles = pltpu.VMEM((lines, LANES), F32)
    a_far, w0_t, w1_t, s_t, ends = pl.pallas_call(
        functools.partial(filter_kernel, *sizes),
        out_shape=[sds((ROOM * lines, LANES))] + [line] * 3 + [sds((4, per, LANES))],
        in_specs=[HBM] * 2,
        out_specs=[HBM] + [VMEM] * 4,
        scratch_shapes=[pltpu.VMEM(flat_control.shape, F32)] * 2
        + [tiles] * 5
        + [
            pltpu.VMEM((2, rows, LANES, LANES), F32),
            pltpu.SemaphoreType.DMA((2 * fields,)),
            pltpu.SemaphoreType.DMA((1,)),
        ],
        compiler_params=params(34),
        cost_estimate=cost(6),
        name="filter_local",
    )(flat_control, flat_smoothing)
    gathered = lax.all_gather(ends, "lon")

    halo_rows = (fields * HALO + 1) * LANES
    halo_shape = sds((halo_rows, LANES), BF)
    first, second, entering = pl.pallas_call(
        functools.partial(edges_kernel, fields, rows, count),
        out_shape=[halo_shape, halo_shape, sds((2, per, LANES))],
        in_specs=[VMEM] * 4,
        out_specs=[VMEM] * 3,
        scratch_shapes=[pltpu.VMEM((2, *halo_shape.shape), BF)],
        compiler_params=params(16),
        cost_estimate=cost(1),
        name="edges",
    )(gathered, w0_t, w1_t, s_t)

    bands = lax.axis_size("lat")
    even = [p for i in range(0, bands - 1, 2) for p in ((i, i + 1), (i + 1, i))]
    odd = [p for i in range(1, bands - 1, 2) for p in ((i, i + 1), (i + 1, i))]
    first = lax.ppermute(first, "lat", even)
    second = lax.ppermute(second, "lat", odd)
    sites = rows * longitudes
    parts = sites // CELLS
    inner_shape = (fields, (parts - 2) * padded, CELLS)
    partial_shape = (blocks, 2 * HALO, longitudes, LANES)
    inner, partial = pl.pallas_call(
        functools.partial(interior_kernel, fields, rows),
        out_shape=[
            sds((FAR * fields, *inner_shape[1:]), BF), sds((FAR * blocks, *partial_shape[1:]))
        ],
        in_specs=[VMEM] * 6,
        out_specs=[HBM] * 2,
        scratch_shapes=[
            pltpu.VMEM(inner_shape, BF),
            pltpu.VMEM(partial_shape, F32),
            pltpu.VMEM((per, longitudes, LANES), F32),
            pltpu.VMEM((blocks, sites - 2 * CELLS, LANES), F32),
            pltpu.SemaphoreType.DMA((fields + 1,)),
        ],
        compiler_params=params(44),
        cost_estimate=cost(3),
        name="interior",
    )(entering, w0_t, w1_t, s_t, taps, vert)

    outward = sds((halo_rows + 2 * count, LANES), BF)
    lift_shape = (blocks, sites, LANES)
    staged = [
        sds(inner_shape, BF), sds(partial_shape), sds(jacobian.shape, BF), sds(vert.shape, BF),
        sds(taps.shape),
    ]
    inner, partial, jacobian, near_vert, near_taps = pl.pallas_call(
        functools.partial(stage_kernel, *sizes),
        out_shape=staged,
        in_specs=[HBM] * 3 + [VMEM] * 2,
        out_specs=[VMEM] * 5,
        scratch_shapes=[
            pltpu.VMEM((fields, padded, 2 * LANES), F32),
            pltpu.SemaphoreType.DMA((3,)),
        ],
        compiler_params=params(44),
        cost_estimate=cost(3),
        name="stage",
    )(
        inner, partial, jacobian,
        jnp.transpose(vert_corr, (1, 0, 2)), jnp.transpose(lat_taps, (1, 0, 2)),
    )
    lift, first, second, *residuals = pl.pallas_call(
        functools.partial(observe_kernel, *sizes, bands),
        out_shape=[sds(lift_shape), outward, outward]
        + [sds((count, slots))] * (bands - 1),
        in_specs=[SMEM] * 3 + [VMEM] * 3 + [HBM] * 2 + [VMEM] * 3,
        out_specs=[VMEM] * (bands + 2),
        scratch_shapes=[
            pltpu.VMEM((fields, parts * padded, CELLS), BF),
            pltpu.VMEM((2, *halo_shape.shape), BF),
            pltpu.VMEM((blocks, 2 * CELLS, LANES), F32),
            pltpu.VMEM((2, *outward.shape), BF),
            pltpu.VMEM(((bands + 1) * count + 8, slots), F32),
            pltpu.SMEM((fields * total,), jnp.int32),
            pltpu.SMEM((fields,), jnp.int32),
            pltpu.SMEM((total // GROUP + fields,), jnp.int32),
            pltpu.SMEM((total // GROUP + fields,), jnp.int32),
            pltpu.VMEM((fields, parts * padded, CELLS), F32),
            pltpu.SemaphoreType.DMA((2,)),
        ],
        compiler_params=params(OBS_MIB),
        cost_estimate=cost(14),
        name="observe",
    )(
        obs_field[0], obs_owner[0], obs_count[0], obs_cell[0],
        inner, partial, first, second, near_taps, near_vert, jacobian,
    )

    swap = [(0, bands - 1), (bands - 1, 0)]
    arrived = [residuals[0], lax.ppermute(residuals[1], "lat", swap)]
    for n in range(2, bands - 1):
        ring = [(i, (i + n) % bands) for i in range(bands)]
        arrived.append(lax.ppermute(residuals[n], "lat", ring))
    first = lax.ppermute(first, "lat", even)
    second = lax.ppermute(second, "lat", odd)
    carried = 2 * per + (bands + 1) * count
    a_again, g_t, gq_t, gp_t, spread = pl.pallas_call(
        functools.partial(respond_kernel, fields, rows),
        out_shape=[line] * 5,
        in_specs=[VMEM, VMEM, HBM],
        out_specs=[VMEM] * 5,
        scratch_shapes=[tiles, pltpu.SemaphoreType.DMA((4,))],
        compiler_params=params(36),
        cost_estimate=cost(5),
        name="respond",
    )(lift, taps, a_far)
    u_t, ends = pl.pallas_call(
        functools.partial(adjoint_kernel, fields, rows),
        out_shape=[line, sds((carried, LANES))],
        in_specs=[VMEM] * (5 + len(arrived)),
        out_specs=[VMEM] * 2,
        scratch_shapes=[tiles] * 2 + [pltpu.VMEM((2, *outward.shape), BF)],
        compiler_params=params(20),
        cost_estimate=cost(3),
        name="adjoint_local",
    )(spread, first, second, a_again, g_t, *arrived)
    gathered_back = lax.all_gather(ends, "lon")
    gradient, returned = pl.pallas_call(
        functools.partial(gradient_kernel, *sizes, count, bands),
        out_shape=[sds(flat_control.shape), sds((total, slots))],
        in_specs=[VMEM] * 6,
        out_specs=[HBM, VMEM],
        scratch_shapes=[
            tiles,
            pltpu.VMEM((rows, LANES, LANES), F32),
            pltpu.VMEM(flat_control.shape, F32),
            pltpu.SemaphoreType.DMA((fields,)),
        ],
        compiler_params=params(20),
        cost_estimate=cost(3),
        name="gradient",
    )(gathered, gathered_back, u_t, gq_t, gp_t, flat_control)
    return gradient.reshape(control.shape), returned[None]


def solution(mesh):
    return jax.shard_map(
        local,
        mesh=mesh,
        in_specs=(
            P(None, None, "lat", "lon"),
            P(None, None, "lat", "lon"),
            P(None, None, "lat"),
            P(),
            P(("lon", "lat"), None, None),
            P(("lon", "lat"), None),
            P(("lon", "lat"), None),
            P(("lon", "lat"), None),
            P(("lon", "lat"), None, None, None),
            P(("lon", "lat"), None, None),
            P(("lon", "lat"), None, None),
        ),
        out_specs=(P(None, None, "lat", "lon"), P(("lon", "lat"), None, None)),
        check_vma=False,
    )
```

```python
import functools

import jax
import jax.numpy as jnp
from jax import lax
from jax.experimental import pallas as pl
from jax.experimental.pallas import tpu as pltpu
from jax.sharding import PartitionSpec as P

LANES = 128
HALO = 2
OBS_MIB = 28
FAR_MIB = 60
ROOM = 12
FAR = 24
CELLS = 256
GROUP = 6
BF = jnp.bfloat16
F32 = jnp.float32
NT = (((1,), (1,)), ((), ()))
TN = (((0,), (0,)), ((), ()))
VMEM = pl.BlockSpec(memory_space=pltpu.VMEM)
SMEM = pl.BlockSpec(memory_space=pltpu.SMEM)
HBM = pl.BlockSpec(memory_space=pltpu.HBM)


def params(mib):
    return pltpu.CompilerParams(vmem_limit_bytes=mib * 1024 * 1024)


def cost(microseconds):
    return pl.CostEstimate(
        flops=0, bytes_accessed=int(microseconds * 3.5e6), transcendentals=0
    )


def sds(shape, dtype=F32):
    return jax.ShapeDtypeStruct(shape, dtype)


def split(x):
    high = x.astype(BF)
    return high, (x - high.astype(F32)).astype(BF)


def step_rows(i, per):
    return pl.ds(pl.multiple_of(i * per, 8), per)


def solve_sectors(me, products, ends, cross, backs):
    count = len(products)
    whole, state = products[0], ends[0]
    for s in range(1, count):
        state = products[s] * state + ends[s]
        whole = whole * products[s]
    gap = 1.0 - whole
    east = state / gap
    east_in = jnp.zeros_like(east)
    turned = []
    for s in range(count):
        east_in = jnp.where(me == s, east, east_in)
        turned.append(backs[s] + cross[s] * east)
        east = products[s] * east + ends[s]
    state = turned[count - 1]
    for s in range(count - 2, -1, -1):
        state = products[s] * state + turned[s]
    west = state / gap
    west_in = jnp.zeros_like(west)
    for s in range(count - 1, -1, -1):
        west_in = jnp.where(me == s, west, west_in)
        west = products[s] * west + turned[s]
    return east_in, west_in


def pile_kernel(*refs):
    for n, ref in enumerate(refs[:-1]):
        refs[-1][n] = ref[...]


def gather_sectors(x):
    count = lax.axis_size("lon")

    def swap(y, mask):
        return lax.ppermute(y, "lon", [(i, i ^ mask) for i in range(count)])

    pieces = [x] + [swap(x, mask) for mask in range(2, count, 2)]
    near = pl.pallas_call(
        pile_kernel,
        out_shape=sds((len(pieces), *x.shape)),
        in_specs=[VMEM] * len(pieces),
        out_specs=VMEM,
        compiler_params=params(8),
        cost_estimate=cost(1),
        name="pile",
    )(*pieces)
    return near, swap(near, 1)


def sector_rows(pair, sector, me, rows):
    near, far = pair
    apart = jnp.bitwise_xor(sector, me)
    return jnp.where(apart % 2 == 0, near[apart // 2, rows], far[apart // 2, rows])


def fetch(pairs, arrived):
    copies = [pltpu.make_async_copy(a, b, arrived.at[n]) for n, (a, b) in enumerate(pairs)]
    for copy in copies:
        copy.start()
    return copies


def pack_kernel(levels, jacobian, value, precision, sent, held, small, wide, ready, arrived, left):
    blocks, padded = sent.shape[:2]
    chunk = held.shape[2]
    copies = fetch(
        [(value, small.at[0]), (precision, small.at[1])]
        + [
            (jacobian.at[:, pl.ds(c * chunk, chunk)], held.at[c])
            for c in range(blocks // chunk)
        ],
        arrived,
    )
    spare = (padded - levels - 2) * chunk
    wide[pl.ds((levels + 2) * chunk, spare), :] = jnp.zeros((spare, LANES), F32)
    copies[0].wait()
    copies[1].wait()
    leaving = []
    for c in range(blocks // chunk):
        copies[2 + c].wait()

        def put(l, _):
            wide[pl.ds(pl.multiple_of(l * chunk, 8), chunk), :] = held[c, l].astype(F32)
            return 0

        lax.fori_loop(0, levels, put, 0, unroll=8)
        for n in range(2):
            part = small[n, pl.ds(c * chunk, chunk), :].astype(F32)
            wide[pl.ds((levels + n) * chunk, chunk), :] = part
        for k in range(chunk):
            ready[c * chunk + k] = wide[pl.ds(k, padded, stride=chunk), :].astype(BF)
        at = pl.ds(c * chunk, chunk)
        leaving += fetch([(ready.at[at], sent.at[at])], left.at[pl.ds(c, 1)])
    for copy in leaving:
        copy.wait()


def prepare_kernel(fields, levels, rows, vert, lat_taps, both, taps, wide):
    over, room = levels - LANES, LANES // fields
    wide[...] = jnp.zeros_like(wide)
    for f in range(fields):
        v = vert[:, f, :]
        wide[f, :levels, :LANES] = v[:, :LANES]
        begin = LANES + f * room
        wide[f, :levels, begin : begin + over] = v[:, LANES:]
    both[:, :, : 2 * LANES], both[:, :, 2 * LANES :] = split(wide[...])
    diagonal = lax.broadcasted_iota(jnp.int32, (rows, rows), 0) == lax.broadcasted_iota(
        jnp.int32, (rows, rows), 1
    )
    lane = lax.broadcasted_iota(jnp.int32, (rows, LANES), 1) // room
    for t in range(2 * HALO + 1):
        last = jnp.zeros((rows, LANES), F32)
        for f in range(fields):
            line = jnp.broadcast_to(lat_taps[t, f : f + 1, :], (rows, rows))
            column = jnp.sum(jnp.where(diagonal, line, 0.0), axis=1, keepdims=True)
            column = jnp.broadcast_to(column, (rows, LANES))
            taps[t, f] = column
            last = jnp.where(lane == f, column, last)
        taps[t, fields] = last


def filter_kernel(
    fields, levels, rows, control, smoothing,
    a_far, w0_t, w1_t, s_t, ends,
    control_v, smoothing_v, a_t, g_t, x_t, e_t, pe_t, extra, arrived, left,
):
    per = (fields + 1) * rows
    over, room = levels - LANES, LANES // fields
    pairs = []
    for f in range(fields):
        at = pl.ds(f * levels * rows, levels * rows)
        pairs.append((smoothing.at[at], smoothing_v.at[at]))
        pairs.append((control.at[at], control_v.at[at]))
    copies = fetch(pairs, arrived)
    extra[...] = jnp.zeros_like(extra)
    for f in range(fields):
        for n, (src, dst) in enumerate(((smoothing_v, a_t), (control_v, x_t))):
            copies[2 * f + n].wait()
            for j in range(rows):
                tile = src[pl.ds(f * levels * rows + j, LANES, stride=rows), :]
                dst[pl.ds(f * rows + j, LANES, stride=per), :] = tile.T
                extra[n, j, pl.ds(f * room, over), :] = src[
                    pl.ds((f * levels + LANES) * rows + j, over, stride=rows), :
                ]
    for j in range(rows):
        at = pl.ds(fields * rows + j, LANES, stride=per)
        a_t[at, :] = extra[0, j].T
        x_t[at, :] = extra[1, j].T

    leaving = fetch([(a_t, a_far.at[pl.ds(0, a_t.shape[0])])], left)

    def east(i, carry):
        e, p = carry
        at = step_rows(i, per)
        a = a_t[at, :]
        g = jnp.sqrt((1.0 - a) * (1.0 + a))
        g_t[at, :] = g
        pe_t[at, :] = p
        e = a * e + g * x_t[at, :]
        e_t[at, :] = e
        return e, p * a

    zero = jnp.zeros((per, LANES), F32)
    one = jnp.ones((per, LANES), F32)
    e, p = lax.fori_loop(0, LANES, east, (zero, one), unroll=4)

    def west(k, carry):
        w0, w1, s = carry
        at = step_rows(LANES - 1 - k, per)
        a, g = a_t[at, :], g_t[at, :]
        w0 = a * w0 + g * e_t[at, :]
        w1 = a * (w1 + g * pe_t[at, :])
        s = a * s
        w0_t[at, :] = w0
        w1_t[at, :] = w1
        s_t[at, :] = s
        return w0, w1, s

    w0, w1, _ = lax.fori_loop(0, LANES, west, (zero, zero, one), unroll=4)
    for n, end in enumerate((p, e, w0, w1)):
        ends[pl.ds(n * per, per), :] = end
    for copy in leaving:
        copy.wait()


def put_halo(dst, b, fields, first, second):
    if b < fields:
        dst[pl.ds(b * HALO * LANES, LANES), :] = first.astype(BF)
        dst[pl.ds((b * HALO + 1) * LANES, LANES), :] = second.astype(BF)
    else:
        half = LANES // fields // 2
        both = first + pltpu.roll(second, half, 1)
        dst[pl.ds(b * HALO * LANES, LANES), :] = both.astype(BF)


def get_halo(src, b, fields):
    first = src[pl.ds(b * HALO * LANES, LANES), :].astype(F32)
    if b < fields:
        return first, src[pl.ds((b * HALO + 1) * LANES, LANES), :].astype(F32)
    return first, pltpu.roll(first, LANES - LANES // fields // 2, 1)


def edges_kernel(fields, rows, count, near, far, w0_t, w1_t, s_t, first, second, entering, sides):
    per = (fields + 1) * rows
    me = lax.axis_index("lon")
    part = [
        [sector_rows((near, far), s, me, pl.ds(q * per, per)) for s in range(count)]
        for q in range(4)
    ]
    east_in, west_in = solve_sectors(me, part[0], part[1], part[3], part[2])
    entering[0] = east_in
    entering[1] = west_in
    odd = lax.axis_index("lat") % 2
    high, low = sides.at[odd], sides.at[1 - odd]
    for b in range(fields + 1):
        for begin, dst in ((b * rows, low), (b * rows + rows - HALO, high)):
            lines = []
            for n in range(begin, begin + HALO):
                at = pl.ds(n, LANES, stride=per)
                line = w0_t[at, :] + w1_t[at, :] * east_in[n : n + 1]
                lines.append(line + s_t[at, :] * west_in[n : n + 1])
            put_halo(dst, b, fields, *lines)
    first[...] = sides[0]
    second[...] = sides[1]


def vertical(vert, mixed):
    padded = vert.shape[0]
    v = jnp.concatenate([vert[:, : 2 * LANES], vert[:, 2 * LANES :]], axis=0)
    high, low = split(mixed)
    out = lax.dot_general(v, high, NT, preferred_element_type=F32)
    out = out[:padded] + out[padded:]
    out += lax.dot_general(v[:padded], low, NT, preferred_element_type=F32)
    return out.astype(BF)


def interior_kernel(
    fields, rows, entering, w0_t, w1_t, s_t, taps, vert, state_far, partial_far,
    state, partial, western, mixed, left,
):
    blocks = fields + 1
    per = blocks * rows
    for n in range(per):
        at = pl.ds(n, LANES, stride=per)
        line = w0_t[at, :] + w1_t[at, :] * entering[0, n : n + 1, :]
        western[n] = line + s_t[at, :] * entering[1, n : n + 1, :]
    for b in range(blocks):
        for j in range(rows):
            total = taps[HALO, b, j : j + 1, :] * western[b * rows + j]
            for t in range(2 * HALO + 1):
                if t != HALO and 0 <= j + t - HALO < rows:
                    total += taps[t, b, j : j + 1, :] * western[b * rows + j + t - HALO]
            if HALO <= j < rows - HALO:
                mixed[b, pl.ds((j - HALO) * LANES, LANES), :] = total
            else:
                partial[b, j if j < HALO else j - rows + 2 * HALO] = total
    padded = vert.shape[1]
    leaving = fetch([(partial, partial_far.at[pl.ds(0, blocks)])], left.at[pl.ds(fields, 1)])
    for f in range(fields):
        for h in range(state.shape[1] // padded):
            at = pl.ds(h * CELLS, CELLS)
            both = jnp.concatenate([mixed[f, at, :], mixed[fields, at, :]], axis=1)
            state[f, pl.ds(h * padded, padded), :] = vertical(vert[f], both)
        leaving += fetch([(state.at[f], state_far.at[f])], left.at[pl.ds(f, 1)])
    for copy in leaving:
        copy.wait()


def stage_kernel(
    fields, levels, rows, inner_far, partial_far, jacobian_far, vert_corr, lat_taps,
    inner, partial, jacobian, vert, taps, wide, arrived,
):
    copies = fetch(
        [
            (jacobian_far, jacobian),
            (partial_far.at[pl.ds(0, fields + 1)], partial),
            (inner_far.at[pl.ds(0, fields)], inner),
        ],
        arrived,
    )
    prepare_kernel(fields, levels, rows, vert_corr, lat_taps, vert, taps, wide)
    for copy in copies:
        copy.wait()


def route_of(delta, bands):
    cyclic = 2 + (delta + bands) % bands
    far = jnp.where(jnp.abs(delta) == bands - 1, 3, cyclic)
    near = jnp.where(delta == 1, 1, jnp.where(delta == -1, 2, 0))
    return jnp.where(jnp.abs(delta) <= 1, near, far)


def observe_kernel(
    fields, levels, rows, bands, field, owner, live, cells,
    inner, partial, first_far, second_far, taps, vert, jacobian, *rest,
):
    lift, first_out, second_out = rest[:3]
    residuals = rest[3 : 2 + bands]
    (
        state, beside, mixed, sides,
        route, order, number, group_field, group_start, acc, arrived,
    ) = rest[2 + bands :]
    blocks = fields + 1
    band = lax.axis_index("lat")
    odd = band % 2
    after, before = beside.at[0], beside.at[1]
    low, high = sides.at[odd], sides.at[1 - odd]
    copies = fetch([(first_far, beside.at[odd]), (second_far, beside.at[1 - odd])], arrived)
    total = field.shape[0]
    padded = vert.shape[1]
    parts = rows * LANES // CELLS
    wide = GROUP * LANES
    sectors = total // bands
    for f in range(fields):
        number[f] = 0

    def place(k, _):
        f = field[k]
        n = number[f]
        order[f * total + n] = k
        number[f] = n + 1
        return 0

    lax.fori_loop(0, total, place, 0)
    groups = 0
    for f in range(fields):
        here = (number[f] + GROUP - 1) // GROUP

        def put(p, _, f=f, first=groups):
            group_field[first + p] = f
            group_start[first + p] = GROUP * p
            return 0

        lax.fori_loop(0, here, put, 0)
        groups = groups + here
    acc[...] = jnp.zeros_like(acc)

    for f in range(fields):
        state[f, pl.ds(padded, (parts - 2) * padded), :] = inner[f]
    for copy in copies:
        copy.wait()

    def tap_of(t, b, j):
        return taps[t, b, j : j + 1, :]

    end = rows - 1
    for b in range(blocks):
        above, below = get_halo(before, b, fields), get_halo(after, b, fields)
        outer_rows = (
            partial[b, 0] + tap_of(0, b, 0) * above[0] + tap_of(1, b, 0) * above[1],
            partial[b, 1] + tap_of(0, b, 1) * above[1],
            partial[b, 2] + tap_of(4, b, end - 1) * below[0],
            partial[b, 3] + tap_of(3, b, end) * below[0] + tap_of(4, b, end) * below[1],
        )
        for n, line in enumerate(outer_rows):
            mixed[b, pl.ds(n * LANES, LANES), :] = line
    for f in range(fields):
        for h in range(2):
            at = pl.ds(h * CELLS, CELLS)
            both = jnp.concatenate([mixed[f, at, :], mixed[fields, at, :]], axis=1)
            state[f, pl.ds(h * (parts - 1) * padded, padded), :] = vertical(vert[f], both)

    site = lax.broadcasted_iota(jnp.int32, (CELLS, wide), 0)
    slot = lax.broadcasted_iota(jnp.int32, (1, LANES), 1)
    spare = (bands + 1) * sectors

    def group(p, _):
        f = group_field[p]
        places, names, at = [], [], []
        for n in range(GROUP):
            b = group_start[p] + n
            known = b < number[f]
            k = jnp.where(known, order[f * total + jnp.where(known, b, 0)], 0)
            count = jnp.where(known, live[k], 0)
            places.append(jnp.where(slot < count, cells[pl.ds(k, 1), :], -1))
            w = owner[k]
            names.append(w)
            to = route_of(w % bands - band, bands) * sectors + w // bands
            at.append(jnp.where(known, to, spare))
        place = jnp.concatenate(places, axis=1)
        part = place // CELLS
        onehot = (site == jnp.where(place < 0, -1, place % CELLS)).astype(F32).astype(BF)
        j = jnp.concatenate([jacobian[w] for w in names], axis=1).astype(F32)
        found_all = jnp.dot(state[f], onehot, preferred_element_type=F32)
        columns = jnp.zeros_like(j)
        for h in range(parts):
            columns = jnp.where(part == h, found_all[h * padded : (h + 1) * padded], columns)
        model = jnp.sum(j * columns, axis=0, keepdims=True)
        value, precision = j[levels : levels + 1], j[levels + 1 : levels + 2]
        res = precision * (model - value)
        adjoint = (j * res).astype(BF)
        adjoint = jnp.concatenate(
            [adjoint * (part == h).astype(F32).astype(BF) for h in range(parts)], axis=0
        )
        for n in range(GROUP):
            route[pl.ds(at[n], 1), :] = res[:, n * LANES : (n + 1) * LANES]
        acc[f] += lax.dot_general(adjoint, onehot, NT, preferred_element_type=F32)
        return 0

    lax.fori_loop(0, groups, group, 0)
    for f in range(fields):
        for h in range(parts):
            forcing = acc[f, pl.ds(h * padded, padded), :].astype(BF)
            out = lax.dot_general(forcing, vert[f], TN, preferred_element_type=F32)
            out = out[:, : 2 * LANES] + out[:, 2 * LANES :]
            at = pl.ds(h * CELLS, CELLS)
            lift[f, at, :] = out[:, :LANES]
            if f == 0:
                lift[fields, at, :] = out[:, LANES:]
            else:
                lift[fields, at, :] += out[:, LANES:]

    for b in range(blocks):
        def line(j):
            return lift[b, pl.ds(j * LANES, LANES), :]

        for dst, first, second in (
            (low, tap_of(3, b, end) * line(end) + tap_of(4, b, end - 1) * line(end - 1),
             tap_of(4, b, end) * line(end)),
            (high, tap_of(0, b, 0) * line(0),
             tap_of(1, b, 0) * line(0) + tap_of(0, b, 1) * line(1)),
        ):
            put_halo(dst, b, fields, first, second)
    riding = (fields * HALO + 1) * LANES
    for n, dst in ((1, low), (2, high)):
        both = jnp.concatenate(split(route[pl.ds(n * sectors, sectors), :]), axis=0)
        dst[pl.ds(riding, 2 * sectors), :] = both
    first_out[...] = sides[0]
    second_out[...] = sides[1]
    for n, dst in enumerate(residuals):
        source = 0 if n == 0 else n + 2
        dst[...] = route[pl.ds(source * sectors, sectors), :]


def respond_kernel(
    fields, rows, lift, taps, a_far, a_t, g_t, gq_t, gp_t, spread, pe_t, arrived
):
    blocks = fields + 1
    per = blocks * rows
    chunks = 4
    span = LANES // chunks
    parts = [pl.ds(c * span * per, span * per) for c in range(chunks)]
    copies = fetch([(a_far.at[at], a_t.at[at]) for at in parts], arrived)

    def east(i, p):
        at = step_rows(i, per)
        a = a_t[at, :]
        g_t[at, :] = jnp.sqrt((1.0 - a) * (1.0 + a))
        pe_t[at, :] = p
        return p * a

    def west(k, carry):
        w1, s = carry
        at = step_rows(LANES - 1 - k, per)
        a, g = a_t[at, :], g_t[at, :]
        t = w1 + g * pe_t[at, :]
        gq_t[at, :] = g * t
        gp_t[at, :] = g * s
        return a * t, a * s

    one = jnp.ones((per, LANES), F32)
    p = one
    for c, copy in enumerate(copies):
        copy.wait()
        p = lax.fori_loop(c * span, (c + 1) * span, east, p, unroll=4)
    lax.fori_loop(0, LANES, west, (jnp.zeros_like(one), one), unroll=4)
    for b in range(blocks):
        for m in range(rows):
            total = taps[HALO, b, m : m + 1, :] * lift[b, pl.ds(m * LANES, LANES), :]
            for t in range(2 * HALO + 1):
                j = m - t + HALO
                if t != HALO and 0 <= j < rows:
                    total += taps[t, b, j : j + 1, :] * lift[b, pl.ds(j * LANES, LANES), :]
            spread[pl.ds(b * rows + m, LANES, stride=per), :] = total


def adjoint_kernel(fields, rows, spread, first, second, a_t, g_t, *rest):
    residuals = rest[:-5]
    u_t, ends, halo, pass_t, beside = rest[-5:]
    odd = lax.axis_index("lat") % 2
    beside[odd] = first[...]
    beside[1 - odd] = second[...]
    high, low = beside.at[0], beside.at[1]
    blocks = fields + 1
    per = blocks * rows
    sectors = residuals[0].shape[0]
    riding = (fields * HALO + 1) * LANES
    parts = [residuals[0][...]]
    for src in (low, high):
        two = src[pl.ds(riding, 2 * sectors), :].astype(F32)
        parts.append(two[:sectors] + two[sectors:])
    parts += [a[...] for a in residuals[1:]]
    for n, part in enumerate(parts):
        ends[pl.ds(2 * per + n * sectors, sectors), :] = part

    for b in range(blocks):
        for src, begin in ((low, b * rows), (high, b * rows + rows - HALO)):
            for n, line in enumerate(get_halo(src, b, fields)):
                halo[pl.ds(begin + n, LANES, stride=per), :] = line
    row = lax.broadcasted_iota(jnp.int32, (per, LANES), 0) % rows
    edge = (row < HALO) | (row >= rows - HALO)

    def east(i, q):
        at = step_rows(i, per)
        t = spread[at, :] + jnp.where(edge, halo[at, :], 0.0) + q
        pass_t[at, :] = g_t[at, :] * t
        return a_t[at, :] * t

    def west(k, p):
        at = step_rows(LANES - 1 - k, per)
        t = pass_t[at, :] + p
        u_t[at, :] = g_t[at, :] * t
        return a_t[at, :] * t

    zero = jnp.zeros((per, LANES), F32)
    ends[:per] = lax.fori_loop(0, LANES, east, zero, unroll=4)
    ends[per : 2 * per] = lax.fori_loop(0, LANES, west, zero, unroll=4)


def gradient_kernel(
    fields, levels, rows, count, bands, near, far, near_back, far_back, u_t, gq_t, gp_t, control,
    gradient, residual, full, extra, held, arrived,
):
    per = (fields + 1) * rows
    over, room = levels - LANES, LANES // fields
    me = lax.axis_index("lon")
    east_in, west_in = solve_sectors(
        me,
        [sector_rows((near, far), s, me, pl.ds(0, per)) for s in range(count)],
        [sector_rows((near_back, far_back), s, me, pl.ds(0, per)) for s in range(count)],
        [sector_rows((near, far), s, me, pl.ds(3 * per, per)) for s in range(count)],
        [sector_rows((near_back, far_back), s, me, pl.ds(per, per)) for s in range(count)],
    )
    for source in range(bands):
        route = route_of(lax.axis_index("lat") - source, bands)
        for s in range(count):
            line = sector_rows(
                (near_back, far_back), s, me, pl.ds(2 * per + route * count + me, 1)
            )
            residual[pl.ds(s * bands + source, 1), :] = line

    def one(i, _):
        at = step_rows(i, per)
        full[at, :] = u_t[at, :] + gq_t[at, :] * east_in + gp_t[at, :] * west_in
        return 0

    lax.fori_loop(0, LANES, one, 0, unroll=8)
    for j in range(rows):
        extra[j] = full[pl.ds(fields * rows + j, LANES, stride=per), :].T
    copies = []
    for f in range(fields):
        for j in range(rows):
            at = pl.ds(f * levels * rows + j, LANES, stride=rows)
            tile = full[pl.ds(f * rows + j, LANES, stride=per), :].T
            held[at, :] = control[at, :] + tile
            at = pl.ds((f * levels + LANES) * rows + j, over, stride=rows)
            held[at, :] = control[at, :] + extra[j, pl.ds(f * room, over), :]
        at = pl.ds(f * levels * rows, levels * rows)
        copies += fetch([(held.at[at], gradient.at[at])], arrived.at[pl.ds(f, 1)])
    for copy in copies:
        copy.wait()


def local(
    control, smoothing, lat_taps, vert_corr, obs_cell, obs_field, obs_count, obs_owner,
    obs_jacobian, obs_value, obs_precision,
):
    fields, levels, rows, longitudes = control.shape
    blocks = fields + 1
    per = blocks * rows
    count = lax.axis_size("lon")
    both = ("lon", "lat")
    total, slots = obs_cell.shape[1:]
    padded = -(-(levels + 2) // 16) * 16
    lines = longitudes * per
    line = sds((lines, LANES))

    sent = pl.pallas_call(
        functools.partial(pack_kernel, levels),
        out_shape=sds((total, padded, slots), BF),
        in_specs=[HBM] * 3,
        out_specs=HBM,
        scratch_shapes=[
            pltpu.VMEM((total // 16, levels, 16, slots), BF),
            pltpu.VMEM((2, total, slots), BF),
            pltpu.VMEM((padded * 16, slots), F32),
            pltpu.VMEM((total, padded, slots), BF),
            pltpu.SemaphoreType.DMA((2 + total // 16,)),
            pltpu.SemaphoreType.DMA((total // 16,)),
        ],
        compiler_params=params(FAR_MIB),
        cost_estimate=cost(3),
        name="pack",
    )(obs_jacobian[0], obs_value[0], obs_precision[0])
    jacobian = lax.all_to_all(sent, both, split_axis=0, concat_axis=0, tiled=True)

    vert_shape = (fields, padded, 4 * LANES)
    vert, taps = pl.pallas_call(
        functools.partial(prepare_kernel, fields, levels, rows),
        out_shape=[sds(vert_shape, BF), sds((2 * HALO + 1, blocks, rows, LANES))],
        in_specs=[VMEM] * 2,
        out_specs=[VMEM] * 2,
        scratch_shapes=[pltpu.VMEM((fields, padded, 2 * LANES), F32)],
        compiler_params=params(8),
        cost_estimate=cost(1),
        name="prepare",
    )(jnp.transpose(vert_corr, (1, 0, 2)), jnp.transpose(lat_taps, (1, 0, 2)))

    flat_control = control.reshape(fields * levels * rows, longitudes)
    flat_smoothing = smoothing.reshape(fields * levels * rows, longitudes)
    sizes = (fields, levels, rows)
    tiles = pltpu.VMEM((lines, LANES), F32)
    a_far, w0_t, w1_t, s_t, ends = pl.pallas_call(
        functools.partial(filter_kernel, *sizes),
        out_shape=[sds((ROOM * lines, LANES))] + [line] * 3 + [sds((4 * per, LANES))],
        in_specs=[HBM] * 2,
        out_specs=[HBM] + [VMEM] * 4,
        scratch_shapes=[pltpu.VMEM(flat_control.shape, F32)] * 2
        + [tiles] * 5
        + [
            pltpu.VMEM((2, rows, LANES, LANES), F32),
            pltpu.SemaphoreType.DMA((2 * fields,)),
            pltpu.SemaphoreType.DMA((1,)),
        ],
        compiler_params=params(34),
        cost_estimate=cost(6),
        name="filter_local",
    )(flat_control, flat_smoothing)
    near, far = gather_sectors(ends)

    halo_rows = (fields * HALO + 1) * LANES
    halo_shape = sds((halo_rows, LANES), BF)
    first, second, entering = pl.pallas_call(
        functools.partial(edges_kernel, fields, rows, count),
        out_shape=[halo_shape, halo_shape, sds((2, per, LANES))],
        in_specs=[VMEM] * 5,
        out_specs=[VMEM] * 3,
        scratch_shapes=[pltpu.VMEM((2, *halo_shape.shape), BF)],
        compiler_params=params(16),
        cost_estimate=cost(1),
        name="edges",
    )(near, far, w0_t, w1_t, s_t)

    bands = lax.axis_size("lat")
    even = [p for i in range(0, bands - 1, 2) for p in ((i, i + 1), (i + 1, i))]
    odd = [p for i in range(1, bands - 1, 2) for p in ((i, i + 1), (i + 1, i))]
    first = lax.ppermute(first, "lat", even)
    second = lax.ppermute(second, "lat", odd)
    sites = rows * longitudes
    parts = sites // CELLS
    inner_shape = (fields, (parts - 2) * padded, CELLS)
    partial_shape = (blocks, 2 * HALO, longitudes, LANES)
    inner, partial = pl.pallas_call(
        functools.partial(interior_kernel, fields, rows),
        out_shape=[
            sds((FAR * fields, *inner_shape[1:]), BF), sds((FAR * blocks, *partial_shape[1:]))
        ],
        in_specs=[VMEM] * 6,
        out_specs=[HBM] * 2,
        scratch_shapes=[
            pltpu.VMEM(inner_shape, BF),
            pltpu.VMEM(partial_shape, F32),
            pltpu.VMEM((per, longitudes, LANES), F32),
            pltpu.VMEM((blocks, sites - 2 * CELLS, LANES), F32),
            pltpu.SemaphoreType.DMA((fields + 1,)),
        ],
        compiler_params=params(44),
        cost_estimate=cost(3),
        name="interior",
    )(entering, w0_t, w1_t, s_t, taps, vert)

    outward = sds((halo_rows + 2 * count, LANES), BF)
    lift_shape = (blocks, sites, LANES)
    staged = [
        sds(inner_shape, BF), sds(partial_shape), sds(jacobian.shape, BF), sds(vert.shape, BF),
        sds(taps.shape),
    ]
    inner, partial, jacobian, near_vert, near_taps = pl.pallas_call(
        functools.partial(stage_kernel, *sizes),
        out_shape=staged,
        in_specs=[HBM] * 3 + [VMEM] * 2,
        out_specs=[VMEM] * 5,
        scratch_shapes=[
            pltpu.VMEM((fields, padded, 2 * LANES), F32),
            pltpu.SemaphoreType.DMA((3,)),
        ],
        compiler_params=params(44),
        cost_estimate=cost(3),
        name="stage",
    )(
        inner, partial, jacobian,
        jnp.transpose(vert_corr, (1, 0, 2)), jnp.transpose(lat_taps, (1, 0, 2)),
    )
    lift, first, second, *residuals = pl.pallas_call(
        functools.partial(observe_kernel, *sizes, bands),
        out_shape=[sds(lift_shape), outward, outward]
        + [sds((count, slots))] * (bands - 1),
        in_specs=[SMEM] * 3 + [VMEM] * 3 + [HBM] * 2 + [VMEM] * 3,
        out_specs=[VMEM] * (bands + 2),
        scratch_shapes=[
            pltpu.VMEM((fields, parts * padded, CELLS), BF),
            pltpu.VMEM((2, *halo_shape.shape), BF),
            pltpu.VMEM((blocks, 2 * CELLS, LANES), F32),
            pltpu.VMEM((2, *outward.shape), BF),
            pltpu.VMEM(((bands + 1) * count + 8, slots), F32),
            pltpu.SMEM((fields * total,), jnp.int32),
            pltpu.SMEM((fields,), jnp.int32),
            pltpu.SMEM((total // GROUP + fields,), jnp.int32),
            pltpu.SMEM((total // GROUP + fields,), jnp.int32),
            pltpu.VMEM((fields, parts * padded, CELLS), F32),
            pltpu.SemaphoreType.DMA((2,)),
        ],
        compiler_params=params(OBS_MIB),
        cost_estimate=cost(14),
        name="observe",
    )(
        obs_field[0], obs_owner[0], obs_count[0], obs_cell[0],
        inner, partial, first, second, near_taps, near_vert, jacobian,
    )

    swap = [(0, bands - 1), (bands - 1, 0)]
    arrived = [residuals[0], lax.ppermute(residuals[1], "lat", swap)]
    for n in range(2, bands - 1):
        ring = [(i, (i + n) % bands) for i in range(bands)]
        arrived.append(lax.ppermute(residuals[n], "lat", ring))
    first = lax.ppermute(first, "lat", even)
    second = lax.ppermute(second, "lat", odd)
    carried = 2 * per + (bands + 1) * count
    a_again, g_t, gq_t, gp_t, spread = pl.pallas_call(
        functools.partial(respond_kernel, fields, rows),
        out_shape=[line] * 5,
        in_specs=[VMEM, VMEM, HBM],
        out_specs=[VMEM] * 5,
        scratch_shapes=[tiles, pltpu.SemaphoreType.DMA((4,))],
        compiler_params=params(36),
        cost_estimate=cost(5),
        name="respond",
    )(lift, taps, a_far)
    u_t, ends = pl.pallas_call(
        functools.partial(adjoint_kernel, fields, rows),
        out_shape=[line, sds((carried, LANES))],
        in_specs=[VMEM] * (5 + len(arrived)),
        out_specs=[VMEM] * 2,
        scratch_shapes=[tiles] * 2 + [pltpu.VMEM((2, *outward.shape), BF)],
        compiler_params=params(20),
        cost_estimate=cost(3),
        name="adjoint_local",
    )(spread, first, second, a_again, g_t, *arrived)
    near_back, far_back = gather_sectors(ends)
    gradient, returned = pl.pallas_call(
        functools.partial(gradient_kernel, *sizes, count, bands),
        out_shape=[sds(flat_control.shape), sds((total, slots))],
        in_specs=[VMEM] * 8,
        out_specs=[HBM, VMEM],
        scratch_shapes=[
            tiles,
            pltpu.VMEM((rows, LANES, LANES), F32),
            pltpu.VMEM(flat_control.shape, F32),
            pltpu.SemaphoreType.DMA((fields,)),
        ],
        compiler_params=params(20),
        cost_estimate=cost(3),
        name="gradient",
    )(near, far, near_back, far_back, u_t, gq_t, gp_t, flat_control)
    return gradient.reshape(control.shape), returned[None]


def solution(mesh):
    return jax.shard_map(
        local,
        mesh=mesh,
        in_specs=(
            P(None, None, "lat", "lon"),
            P(None, None, "lat", "lon"),
            P(None, None, "lat"),
            P(),
            P(("lon", "lat"), None, None),
            P(("lon", "lat"), None),
            P(("lon", "lat"), None),
            P(("lon", "lat"), None),
            P(("lon", "lat"), None, None, None),
            P(("lon", "lat"), None, None),
            P(("lon", "lat"), None, None),
        ),
        out_specs=(P(None, None, "lat", "lon"), P(("lon", "lat"), None, None)),
        check_vma=False,
    )
```

```python
import functools

import jax
import jax.numpy as jnp
from jax import lax
from jax.experimental import pallas as pl
from jax.experimental.pallas import tpu as pltpu
from jax.sharding import PartitionSpec as P

LANES = 128
HALO = 2
OBS_MIB = 28
FAR_MIB = 60
ROOM = 12
FAR = 24
CELLS = 256
GROUP = 6
BF = jnp.bfloat16
F32 = jnp.float32
NT = (((1,), (1,)), ((), ()))
TN = (((0,), (0,)), ((), ()))
VMEM = pl.BlockSpec(memory_space=pltpu.VMEM)
SMEM = pl.BlockSpec(memory_space=pltpu.SMEM)
HBM = pl.BlockSpec(memory_space=pltpu.HBM)


def params(mib):
    return pltpu.CompilerParams(vmem_limit_bytes=mib * 1024 * 1024)


def cost(microseconds):
    return pl.CostEstimate(
        flops=0, bytes_accessed=int(microseconds * 3.5e6), transcendentals=0
    )


def sds(shape, dtype=F32):
    return jax.ShapeDtypeStruct(shape, dtype)


def split(x):
    high = x.astype(BF)
    return high, (x - high.astype(F32)).astype(BF)


def step_rows(i, per):
    return pl.ds(pl.multiple_of(i * per, 8), per)


def solve_sectors(me, products, ends, cross, backs):
    count = len(products)
    whole, state = products[0], ends[0]
    for s in range(1, count):
        state = products[s] * state + ends[s]
        whole = whole * products[s]
    gap = 1.0 - whole
    east = state / gap
    east_in = jnp.zeros_like(east)
    turned = []
    for s in range(count):
        east_in = jnp.where(me == s, east, east_in)
        turned.append(backs[s] + cross[s] * east)
        east = products[s] * east + ends[s]
    state = turned[count - 1]
    for s in range(count - 2, -1, -1):
        state = products[s] * state + turned[s]
    west = state / gap
    west_in = jnp.zeros_like(west)
    for s in range(count - 1, -1, -1):
        west_in = jnp.where(me == s, west, west_in)
        west = products[s] * west + turned[s]
    return east_in, west_in


def pile_kernel(*refs):
    for n, ref in enumerate(refs[:-1]):
        refs[-1][n] = ref[...]


def gather_sectors(x):
    count = lax.axis_size("lon")

    def swap(y, mask):
        return lax.ppermute(y, "lon", [(i, i ^ mask) for i in range(count)])

    pieces = [x] + [swap(x, mask) for mask in range(2, count, 2)]
    near = pl.pallas_call(
        pile_kernel,
        out_shape=sds((len(pieces), *x.shape)),
        in_specs=[VMEM] * len(pieces),
        out_specs=VMEM,
        compiler_params=params(8),
        cost_estimate=cost(1),
        name="pile",
    )(*pieces)
    return near, swap(near, 1)


def sector_rows(pair, sector, me, rows):
    near, far = pair
    apart = jnp.bitwise_xor(sector, me)
    return jnp.where(apart % 2 == 0, near[apart // 2, rows], far[apart // 2, rows])


def fetch(pairs, arrived):
    copies = [pltpu.make_async_copy(a, b, arrived.at[n]) for n, (a, b) in enumerate(pairs)]
    for copy in copies:
        copy.start()
    return copies


def pack_kernel(levels, jacobian, value, precision, sent, held, small, wide, ready, arrived, left):
    blocks, padded = sent.shape[:2]
    chunk = held.shape[2]
    copies = fetch(
        [(value, small.at[0]), (precision, small.at[1])]
        + [
            (jacobian.at[:, pl.ds(c * chunk, chunk)], held.at[c])
            for c in range(blocks // chunk)
        ],
        arrived,
    )
    spare = (padded - levels - 2) * chunk
    wide[pl.ds((levels + 2) * chunk, spare), :] = jnp.zeros((spare, LANES), F32)
    copies[0].wait()
    copies[1].wait()
    leaving = []
    for c in range(blocks // chunk):
        copies[2 + c].wait()

        def put(l, _):
            wide[pl.ds(pl.multiple_of(l * chunk, 8), chunk), :] = held[c, l].astype(F32)
            return 0

        lax.fori_loop(0, levels, put, 0, unroll=8)
        for n in range(2):
            part = small[n, pl.ds(c * chunk, chunk), :].astype(F32)
            wide[pl.ds((levels + n) * chunk, chunk), :] = part
        for k in range(chunk):
            ready[c * chunk + k] = wide[pl.ds(k, padded, stride=chunk), :].astype(BF)
        at = pl.ds(c * chunk, chunk)
        leaving += fetch([(ready.at[at], sent.at[at])], left.at[pl.ds(c, 1)])
    for copy in leaving:
        copy.wait()


def prepare_kernel(fields, levels, rows, vert, lat_taps, both, taps, wide):
    over, room = levels - LANES, LANES // fields
    wide[...] = jnp.zeros_like(wide)
    for f in range(fields):
        v = vert[:, f, :]
        wide[f, :levels, :LANES] = v[:, :LANES]
        begin = LANES + f * room
        wide[f, :levels, begin : begin + over] = v[:, LANES:]
    both[:, :, : 2 * LANES], both[:, :, 2 * LANES :] = split(wide[...])
    diagonal = lax.broadcasted_iota(jnp.int32, (rows, rows), 0) == lax.broadcasted_iota(
        jnp.int32, (rows, rows), 1
    )
    lane = lax.broadcasted_iota(jnp.int32, (rows, LANES), 1) // room
    for t in range(2 * HALO + 1):
        last = jnp.zeros((rows, LANES), F32)
        for f in range(fields):
            line = jnp.broadcast_to(lat_taps[t, f : f + 1, :], (rows, rows))
            column = jnp.sum(jnp.where(diagonal, line, 0.0), axis=1, keepdims=True)
            column = jnp.broadcast_to(column, (rows, LANES))
            taps[t, f] = column
            last = jnp.where(lane == f, column, last)
        taps[t, fields] = last


def filter_kernel(
    fields, levels, rows, control, smoothing,
    a_far, w0_t, w1_t, s_t, ends,
    control_v, smoothing_v, a_t, g_t, x_t, e_t, pe_t, extra, arrived, left,
):
    per = (fields + 1) * rows
    over, room = levels - LANES, LANES // fields
    pairs = []
    for f in range(fields):
        at = pl.ds(f * levels * rows, levels * rows)
        pairs.append((smoothing.at[at], smoothing_v.at[at]))
        pairs.append((control.at[at], control_v.at[at]))
    copies = fetch(pairs, arrived)
    extra[...] = jnp.zeros_like(extra)
    for f in range(fields):
        for n, (src, dst) in enumerate(((smoothing_v, a_t), (control_v, x_t))):
            copies[2 * f + n].wait()
            for j in range(rows):
                tile = src[pl.ds(f * levels * rows + j, LANES, stride=rows), :]
                dst[pl.ds(f * rows + j, LANES, stride=per), :] = tile.T
                extra[n, j, pl.ds(f * room, over), :] = src[
                    pl.ds((f * levels + LANES) * rows + j, over, stride=rows), :
                ]
    for j in range(rows):
        at = pl.ds(fields * rows + j, LANES, stride=per)
        a_t[at, :] = extra[0, j].T
        x_t[at, :] = extra[1, j].T

    leaving = fetch([(a_t, a_far.at[pl.ds(0, a_t.shape[0])])], left)

    def east(i, carry):
        e, p = carry
        at = step_rows(i, per)
        a = a_t[at, :]
        g = jnp.sqrt((1.0 - a) * (1.0 + a))
        g_t[at, :] = g
        pe_t[at, :] = p
        e = a * e + g * x_t[at, :]
        e_t[at, :] = e
        return e, p * a

    zero = jnp.zeros((per, LANES), F32)
    one = jnp.ones((per, LANES), F32)
    e, p = lax.fori_loop(0, LANES, east, (zero, one), unroll=4)

    def west(k, carry):
        w0, w1, s = carry
        at = step_rows(LANES - 1 - k, per)
        a, g = a_t[at, :], g_t[at, :]
        w0 = a * w0 + g * e_t[at, :]
        w1 = a * (w1 + g * pe_t[at, :])
        s = a * s
        w0_t[at, :] = w0
        w1_t[at, :] = w1
        s_t[at, :] = s
        return w0, w1, s

    w0, w1, _ = lax.fori_loop(0, LANES, west, (zero, zero, one), unroll=4)
    for n, end in enumerate((p, e, w0, w1)):
        ends[pl.ds(n * per, per), :] = end
    for copy in leaving:
        copy.wait()


def put_halo(dst, b, fields, first, second):
    if b < fields:
        dst[pl.ds(b * HALO * LANES, LANES), :] = first.astype(BF)
        dst[pl.ds((b * HALO + 1) * LANES, LANES), :] = second.astype(BF)
    else:
        half = LANES // fields // 2
        both = first + pltpu.roll(second, half, 1)
        dst[pl.ds(b * HALO * LANES, LANES), :] = both.astype(BF)


def get_halo(src, b, fields):
    first = src[pl.ds(b * HALO * LANES, LANES), :].astype(F32)
    if b < fields:
        return first, src[pl.ds((b * HALO + 1) * LANES, LANES), :].astype(F32)
    return first, pltpu.roll(first, LANES - LANES // fields // 2, 1)


def edges_kernel(fields, rows, count, near, far, w0_t, w1_t, s_t, first, second, entering, sides):
    per = (fields + 1) * rows
    me = lax.axis_index("lon")
    part = [
        [sector_rows((near, far), s, me, pl.ds(q * per, per)) for s in range(count)]
        for q in range(4)
    ]
    east_in, west_in = solve_sectors(me, part[0], part[1], part[3], part[2])
    entering[0] = east_in
    entering[1] = west_in
    odd = lax.axis_index("lat") % 2
    high, low = sides.at[odd], sides.at[1 - odd]
    for b in range(fields + 1):
        for begin, dst in ((b * rows, low), (b * rows + rows - HALO, high)):
            lines = []
            for n in range(begin, begin + HALO):
                at = pl.ds(n, LANES, stride=per)
                line = w0_t[at, :] + w1_t[at, :] * east_in[n : n + 1]
                lines.append(line + s_t[at, :] * west_in[n : n + 1])
            put_halo(dst, b, fields, *lines)
    first[...] = sides[0]
    second[...] = sides[1]


def vertical(vert, mixed):
    padded = vert.shape[0]
    v = jnp.concatenate([vert[:, : 2 * LANES], vert[:, 2 * LANES :]], axis=0)
    high, low = split(mixed)
    out = lax.dot_general(v, high, NT, preferred_element_type=F32)
    out = out[:padded] + out[padded:]
    out += lax.dot_general(v[:padded], low, NT, preferred_element_type=F32)
    return out.astype(BF)


def interior_kernel(
    fields, rows, entering, w0_t, w1_t, s_t, taps, vert, state_far, partial_far,
    state, partial, western, mixed, left,
):
    blocks = fields + 1
    per = blocks * rows
    for n in range(per):
        at = pl.ds(n, LANES, stride=per)
        line = w0_t[at, :] + w1_t[at, :] * entering[0, n : n + 1, :]
        western[n] = line + s_t[at, :] * entering[1, n : n + 1, :]
    for b in range(blocks):
        for j in range(rows):
            total = taps[HALO, b, j : j + 1, :] * western[b * rows + j]
            for t in range(2 * HALO + 1):
                if t != HALO and 0 <= j + t - HALO < rows:
                    total += taps[t, b, j : j + 1, :] * western[b * rows + j + t - HALO]
            if HALO <= j < rows - HALO:
                mixed[b, pl.ds((j - HALO) * LANES, LANES), :] = total
            else:
                partial[b, j if j < HALO else j - rows + 2 * HALO] = total
    padded = vert.shape[1]
    leaving = fetch([(partial, partial_far.at[pl.ds(0, blocks)])], left.at[pl.ds(fields, 1)])
    for f in range(fields):
        for h in range(state.shape[1] // padded):
            at = pl.ds(h * CELLS, CELLS)
            both = jnp.concatenate([mixed[f, at, :], mixed[fields, at, :]], axis=1)
            state[f, pl.ds(h * padded, padded), :] = vertical(vert[f], both)
        leaving += fetch([(state.at[f], state_far.at[f])], left.at[pl.ds(f, 1)])
    for copy in leaving:
        copy.wait()


def stage_kernel(
    fields, levels, rows, inner_far, partial_far, jacobian_far, vert_corr, lat_taps,
    inner, partial, jacobian, vert, taps, wide, arrived,
):
    copies = fetch(
        [
            (jacobian_far, jacobian),
            (partial_far.at[pl.ds(0, fields + 1)], partial),
            (inner_far.at[pl.ds(0, fields)], inner),
        ],
        arrived,
    )
    prepare_kernel(fields, levels, rows, vert_corr, lat_taps, vert, taps, wide)
    for copy in copies:
        copy.wait()


def route_of(delta, bands):
    cyclic = 2 + (delta + bands) % bands
    far = jnp.where(jnp.abs(delta) == bands - 1, 3, cyclic)
    near = jnp.where(delta == 1, 1, jnp.where(delta == -1, 2, 0))
    return jnp.where(jnp.abs(delta) <= 1, near, far)


def observe_kernel(
    fields, levels, rows, bands, field, owner, live, cells,
    inner, partial, first_far, second_far, taps, vert, jacobian, *rest,
):
    lift, first_out, second_out = rest[:3]
    residuals = rest[3 : 2 + bands]
    (
        state, beside, mixed, sides,
        route, order, number, group_field, group_start, acc, arrived,
    ) = rest[2 + bands :]
    blocks = fields + 1
    band = lax.axis_index("lat")
    odd = band % 2
    after, before = beside.at[0], beside.at[1]
    low, high = sides.at[odd], sides.at[1 - odd]
    copies = fetch([(first_far, beside.at[odd]), (second_far, beside.at[1 - odd])], arrived)
    total = field.shape[0]
    padded = vert.shape[1]
    parts = rows * LANES // CELLS
    wide = GROUP * LANES
    sectors = total // bands
    for f in range(fields):
        number[f] = 0

    def place(k, _):
        f = field[k]
        n = number[f]
        order[f * total + n] = k
        number[f] = n + 1
        return 0

    lax.fori_loop(0, total, place, 0)
    groups = 0
    for f in range(fields):
        here = (number[f] + GROUP - 1) // GROUP

        def put(p, _, f=f, first=groups):
            group_field[first + p] = f
            group_start[first + p] = GROUP * p
            return 0

        lax.fori_loop(0, here, put, 0)
        groups = groups + here
    acc[...] = jnp.zeros_like(acc)

    for f in range(fields):
        state[f, pl.ds(padded, (parts - 2) * padded), :] = inner[f]
    for copy in copies:
        copy.wait()

    def tap_of(t, b, j):
        return taps[t, b, j : j + 1, :]

    end = rows - 1
    for b in range(blocks):
        above, below = get_halo(before, b, fields), get_halo(after, b, fields)
        outer_rows = (
            partial[b, 0] + tap_of(0, b, 0) * above[0] + tap_of(1, b, 0) * above[1],
            partial[b, 1] + tap_of(0, b, 1) * above[1],
            partial[b, 2] + tap_of(4, b, end - 1) * below[0],
            partial[b, 3] + tap_of(3, b, end) * below[0] + tap_of(4, b, end) * below[1],
        )
        for n, line in enumerate(outer_rows):
            mixed[b, pl.ds(n * LANES, LANES), :] = line
    for f in range(fields):
        for h in range(2):
            at = pl.ds(h * CELLS, CELLS)
            both = jnp.concatenate([mixed[f, at, :], mixed[fields, at, :]], axis=1)
            state[f, pl.ds(h * (parts - 1) * padded, padded), :] = vertical(vert[f], both)

    site = lax.broadcasted_iota(jnp.int32, (CELLS, wide), 0)
    slot = lax.broadcasted_iota(jnp.int32, (1, LANES), 1)
    spare = (bands + 1) * sectors

    def group(p, _):
        f = group_field[p]
        places, names, at = [], [], []
        for n in range(GROUP):
            b = group_start[p] + n
            known = b < number[f]
            k = jnp.where(known, order[f * total + jnp.where(known, b, 0)], 0)
            count = jnp.where(known, live[k], 0)
            places.append(jnp.where(slot < count, cells[pl.ds(k, 1), :], -1))
            w = owner[k]
            names.append(w)
            to = route_of(w % bands - band, bands) * sectors + w // bands
            at.append(jnp.where(known, to, spare))
        place = jnp.concatenate(places, axis=1)
        part = place // CELLS
        onehot = (site == jnp.where(place < 0, -1, place % CELLS)).astype(F32).astype(BF)
        j = jnp.concatenate([jacobian[w] for w in names], axis=1).astype(F32)
        found_all = jnp.dot(state[f], onehot, preferred_element_type=F32)
        columns = jnp.zeros_like(j)
        for h in range(parts):
            columns = jnp.where(part == h, found_all[h * padded : (h + 1) * padded], columns)
        model = jnp.sum(j * columns, axis=0, keepdims=True)
        value, precision = j[levels : levels + 1], j[levels + 1 : levels + 2]
        res = precision * (model - value)
        adjoint = (j * res).astype(BF)
        adjoint = jnp.concatenate(
            [adjoint * (part == h).astype(F32).astype(BF) for h in range(parts)], axis=0
        )
        for n in range(GROUP):
            route[pl.ds(at[n], 1), :] = res[:, n * LANES : (n + 1) * LANES]
        acc[f] += lax.dot_general(adjoint, onehot, NT, preferred_element_type=F32)
        return 0

    lax.fori_loop(0, groups, group, 0)
    for f in range(fields):
        for h in range(parts):
            forcing = acc[f, pl.ds(h * padded, padded), :].astype(BF)
            out = lax.dot_general(forcing, vert[f], TN, preferred_element_type=F32)
            out = out[:, : 2 * LANES] + out[:, 2 * LANES :]
            at = pl.ds(h * CELLS, CELLS)
            lift[f, at, :] = out[:, :LANES]
            if f == 0:
                lift[fields, at, :] = out[:, LANES:]
            else:
                lift[fields, at, :] += out[:, LANES:]

    for b in range(blocks):
        def line(j):
            return lift[b, pl.ds(j * LANES, LANES), :]

        for dst, first, second in (
            (low, tap_of(3, b, end) * line(end) + tap_of(4, b, end - 1) * line(end - 1),
             tap_of(4, b, end) * line(end)),
            (high, tap_of(0, b, 0) * line(0),
             tap_of(1, b, 0) * line(0) + tap_of(0, b, 1) * line(1)),
        ):
            put_halo(dst, b, fields, first, second)
    riding = (fields * HALO + 1) * LANES
    for n, dst in ((1, low), (2, high)):
        both = jnp.concatenate(split(route[pl.ds(n * sectors, sectors), :]), axis=0)
        dst[pl.ds(riding, 2 * sectors), :] = both
    first_out[...] = sides[0]
    second_out[...] = sides[1]
    for n, dst in enumerate(residuals):
        source = 0 if n == 0 else n + 2
        dst[...] = route[pl.ds(source * sectors, sectors), :]


def respond_kernel(
    fields, rows, lift, taps, a_far, a_t, g_t, gq_t, gp_t, spread, pe_t, arrived
):
    blocks = fields + 1
    per = blocks * rows
    chunks = 4
    span = LANES // chunks
    parts = [pl.ds(c * span * per, span * per) for c in range(chunks)]
    copies = fetch([(a_far.at[at], a_t.at[at]) for at in parts], arrived)

    def east(i, p):
        at = step_rows(i, per)
        a = a_t[at, :]
        g_t[at, :] = jnp.sqrt((1.0 - a) * (1.0 + a))
        pe_t[at, :] = p
        return p * a

    def west(k, carry):
        w1, s = carry
        at = step_rows(LANES - 1 - k, per)
        a, g = a_t[at, :], g_t[at, :]
        t = w1 + g * pe_t[at, :]
        gq_t[at, :] = g * t
        gp_t[at, :] = g * s
        return a * t, a * s

    for b in range(blocks):
        for m in range(rows):
            total = taps[HALO, b, m : m + 1, :] * lift[b, pl.ds(m * LANES, LANES), :]
            for t in range(2 * HALO + 1):
                j = m - t + HALO
                if t != HALO and 0 <= j < rows:
                    total += taps[t, b, j : j + 1, :] * lift[b, pl.ds(j * LANES, LANES), :]
            spread[pl.ds(b * rows + m, LANES, stride=per), :] = total
    one = jnp.ones((per, LANES), F32)
    p = one
    for c, copy in enumerate(copies):
        copy.wait()
        p = lax.fori_loop(c * span, (c + 1) * span, east, p, unroll=4)
    lax.fori_loop(0, LANES, west, (jnp.zeros_like(one), one), unroll=4)


def adjoint_kernel(fields, rows, spread, first, second, a_t, g_t, *rest):
    residuals = rest[:-5]
    u_t, ends, halo, pass_t, beside = rest[-5:]
    odd = lax.axis_index("lat") % 2
    beside[odd] = first[...]
    beside[1 - odd] = second[...]
    high, low = beside.at[0], beside.at[1]
    blocks = fields + 1
    per = blocks * rows
    sectors = residuals[0].shape[0]
    riding = (fields * HALO + 1) * LANES
    parts = [residuals[0][...]]
    for src in (low, high):
        two = src[pl.ds(riding, 2 * sectors), :].astype(F32)
        parts.append(two[:sectors] + two[sectors:])
    parts += [a[...] for a in residuals[1:]]
    for n, part in enumerate(parts):
        ends[pl.ds(2 * per + n * sectors, sectors), :] = part

    for b in range(blocks):
        for src, begin in ((low, b * rows), (high, b * rows + rows - HALO)):
            for n, line in enumerate(get_halo(src, b, fields)):
                halo[pl.ds(begin + n, LANES, stride=per), :] = line
    row = lax.broadcasted_iota(jnp.int32, (per, LANES), 0) % rows
    edge = (row < HALO) | (row >= rows - HALO)

    def east(i, q):
        at = step_rows(i, per)
        t = spread[at, :] + jnp.where(edge, halo[at, :], 0.0) + q
        pass_t[at, :] = g_t[at, :] * t
        return a_t[at, :] * t

    def west(k, p):
        at = step_rows(LANES - 1 - k, per)
        t = pass_t[at, :] + p
        u_t[at, :] = g_t[at, :] * t
        return a_t[at, :] * t

    zero = jnp.zeros((per, LANES), F32)
    ends[:per] = lax.fori_loop(0, LANES, east, zero, unroll=4)
    ends[per : 2 * per] = lax.fori_loop(0, LANES, west, zero, unroll=4)


def gradient_kernel(
    fields, levels, rows, count, bands, near, far, near_back, far_back, u_t, gq_t, gp_t, control,
    gradient, residual, full, extra, held, arrived,
):
    per = (fields + 1) * rows
    over, room = levels - LANES, LANES // fields
    me = lax.axis_index("lon")
    east_in, west_in = solve_sectors(
        me,
        [sector_rows((near, far), s, me, pl.ds(0, per)) for s in range(count)],
        [sector_rows((near_back, far_back), s, me, pl.ds(0, per)) for s in range(count)],
        [sector_rows((near, far), s, me, pl.ds(3 * per, per)) for s in range(count)],
        [sector_rows((near_back, far_back), s, me, pl.ds(per, per)) for s in range(count)],
    )
    for source in range(bands):
        route = route_of(lax.axis_index("lat") - source, bands)
        for s in range(count):
            line = sector_rows(
                (near_back, far_back), s, me, pl.ds(2 * per + route * count + me, 1)
            )
            residual[pl.ds(s * bands + source, 1), :] = line

    def one(i, _):
        at = step_rows(i, per)
        full[at, :] = u_t[at, :] + gq_t[at, :] * east_in + gp_t[at, :] * west_in
        return 0

    lax.fori_loop(0, LANES, one, 0, unroll=8)
    for j in range(rows):
        extra[j] = full[pl.ds(fields * rows + j, LANES, stride=per), :].T
    copies = []
    for f in range(fields):
        for j in range(rows):
            at = pl.ds(f * levels * rows + j, LANES, stride=rows)
            tile = full[pl.ds(f * rows + j, LANES, stride=per), :].T
            held[at, :] = control[at, :] + tile
            at = pl.ds((f * levels + LANES) * rows + j, over, stride=rows)
            held[at, :] = control[at, :] + extra[j, pl.ds(f * room, over), :]
        at = pl.ds(f * levels * rows, levels * rows)
        copies += fetch([(held.at[at], gradient.at[at])], arrived.at[pl.ds(f, 1)])
    for copy in copies:
        copy.wait()


def local(
    control, smoothing, lat_taps, vert_corr, obs_cell, obs_field, obs_count, obs_owner,
    obs_jacobian, obs_value, obs_precision,
):
    fields, levels, rows, longitudes = control.shape
    blocks = fields + 1
    per = blocks * rows
    count = lax.axis_size("lon")
    both = ("lon", "lat")
    total, slots = obs_cell.shape[1:]
    padded = -(-(levels + 2) // 16) * 16
    lines = longitudes * per
    line = sds((lines, LANES))

    sent = pl.pallas_call(
        functools.partial(pack_kernel, levels),
        out_shape=sds((total, padded, slots), BF),
        in_specs=[HBM] * 3,
        out_specs=HBM,
        scratch_shapes=[
            pltpu.VMEM((total // 16, levels, 16, slots), BF),
            pltpu.VMEM((2, total, slots), BF),
            pltpu.VMEM((padded * 16, slots), F32),
            pltpu.VMEM((total, padded, slots), BF),
            pltpu.SemaphoreType.DMA((2 + total // 16,)),
            pltpu.SemaphoreType.DMA((total // 16,)),
        ],
        compiler_params=params(FAR_MIB),
        cost_estimate=cost(3),
        name="pack",
    )(obs_jacobian[0], obs_value[0], obs_precision[0])
    jacobian = lax.all_to_all(sent, both, split_axis=0, concat_axis=0, tiled=True)

    vert_shape = (fields, padded, 4 * LANES)
    vert, taps = pl.pallas_call(
        functools.partial(prepare_kernel, fields, levels, rows),
        out_shape=[sds(vert_shape, BF), sds((2 * HALO + 1, blocks, rows, LANES))],
        in_specs=[VMEM] * 2,
        out_specs=[VMEM] * 2,
        scratch_shapes=[pltpu.VMEM((fields, padded, 2 * LANES), F32)],
        compiler_params=params(8),
        cost_estimate=cost(1),
        name="prepare",
    )(jnp.transpose(vert_corr, (1, 0, 2)), jnp.transpose(lat_taps, (1, 0, 2)))

    flat_control = control.reshape(fields * levels * rows, longitudes)
    flat_smoothing = smoothing.reshape(fields * levels * rows, longitudes)
    sizes = (fields, levels, rows)
    tiles = pltpu.VMEM((lines, LANES), F32)
    a_far, w0_t, w1_t, s_t, ends = pl.pallas_call(
        functools.partial(filter_kernel, *sizes),
        out_shape=[sds((ROOM * lines, LANES))] + [line] * 3 + [sds((4 * per, LANES))],
        in_specs=[HBM] * 2,
        out_specs=[HBM] + [VMEM] * 4,
        scratch_shapes=[pltpu.VMEM(flat_control.shape, F32)] * 2
        + [tiles] * 5
        + [
            pltpu.VMEM((2, rows, LANES, LANES), F32),
            pltpu.SemaphoreType.DMA((2 * fields,)),
            pltpu.SemaphoreType.DMA((1,)),
        ],
        compiler_params=params(34),
        cost_estimate=cost(6),
        name="filter_local",
    )(flat_control, flat_smoothing)
    near, far = gather_sectors(ends)

    halo_rows = (fields * HALO + 1) * LANES
    halo_shape = sds((halo_rows, LANES), BF)
    first, second, entering = pl.pallas_call(
        functools.partial(edges_kernel, fields, rows, count),
        out_shape=[halo_shape, halo_shape, sds((2, per, LANES))],
        in_specs=[VMEM] * 5,
        out_specs=[VMEM] * 3,
        scratch_shapes=[pltpu.VMEM((2, *halo_shape.shape), BF)],
        compiler_params=params(16),
        cost_estimate=cost(1),
        name="edges",
    )(near, far, w0_t, w1_t, s_t)

    bands = lax.axis_size("lat")
    even = [p for i in range(0, bands - 1, 2) for p in ((i, i + 1), (i + 1, i))]
    odd = [p for i in range(1, bands - 1, 2) for p in ((i, i + 1), (i + 1, i))]
    first = lax.ppermute(first, "lat", even)
    second = lax.ppermute(second, "lat", odd)
    sites = rows * longitudes
    parts = sites // CELLS
    inner_shape = (fields, (parts - 2) * padded, CELLS)
    partial_shape = (blocks, 2 * HALO, longitudes, LANES)
    inner, partial = pl.pallas_call(
        functools.partial(interior_kernel, fields, rows),
        out_shape=[
            sds((FAR * fields, *inner_shape[1:]), BF), sds((FAR * blocks, *partial_shape[1:]))
        ],
        in_specs=[VMEM] * 6,
        out_specs=[HBM] * 2,
        scratch_shapes=[
            pltpu.VMEM(inner_shape, BF),
            pltpu.VMEM(partial_shape, F32),
            pltpu.VMEM((per, longitudes, LANES), F32),
            pltpu.VMEM((blocks, sites - 2 * CELLS, LANES), F32),
            pltpu.SemaphoreType.DMA((fields + 1,)),
        ],
        compiler_params=params(44),
        cost_estimate=cost(3),
        name="interior",
    )(entering, w0_t, w1_t, s_t, taps, vert)

    outward = sds((halo_rows + 2 * count, LANES), BF)
    lift_shape = (blocks, sites, LANES)
    staged = [
        sds(inner_shape, BF), sds(partial_shape), sds(jacobian.shape, BF), sds(vert.shape, BF),
        sds(taps.shape),
    ]
    inner, partial, jacobian, near_vert, near_taps = pl.pallas_call(
        functools.partial(stage_kernel, *sizes),
        out_shape=staged,
        in_specs=[HBM] * 3 + [VMEM] * 2,
        out_specs=[VMEM] * 5,
        scratch_shapes=[
            pltpu.VMEM((fields, padded, 2 * LANES), F32),
            pltpu.SemaphoreType.DMA((3,)),
        ],
        compiler_params=params(44),
        cost_estimate=cost(3),
        name="stage",
    )(
        inner, partial, jacobian,
        jnp.transpose(vert_corr, (1, 0, 2)), jnp.transpose(lat_taps, (1, 0, 2)),
    )
    lift, first, second, *residuals = pl.pallas_call(
        functools.partial(observe_kernel, *sizes, bands),
        out_shape=[sds(lift_shape), outward, outward]
        + [sds((count, slots))] * (bands - 1),
        in_specs=[SMEM] * 3 + [VMEM] * 3 + [HBM] * 2 + [VMEM] * 3,
        out_specs=[VMEM] * (bands + 2),
        scratch_shapes=[
            pltpu.VMEM((fields, parts * padded, CELLS), BF),
            pltpu.VMEM((2, *halo_shape.shape), BF),
            pltpu.VMEM((blocks, 2 * CELLS, LANES), F32),
            pltpu.VMEM((2, *outward.shape), BF),
            pltpu.VMEM(((bands + 1) * count + 8, slots), F32),
            pltpu.SMEM((fields * total,), jnp.int32),
            pltpu.SMEM((fields,), jnp.int32),
            pltpu.SMEM((total // GROUP + fields,), jnp.int32),
            pltpu.SMEM((total // GROUP + fields,), jnp.int32),
            pltpu.VMEM((fields, parts * padded, CELLS), F32),
            pltpu.SemaphoreType.DMA((2,)),
        ],
        compiler_params=params(OBS_MIB),
        cost_estimate=cost(14),
        name="observe",
    )(
        obs_field[0], obs_owner[0], obs_count[0], obs_cell[0],
        inner, partial, first, second, near_taps, near_vert, jacobian,
    )

    swap = [(0, bands - 1), (bands - 1, 0)]
    arrived = [residuals[0], lax.ppermute(residuals[1], "lat", swap)]
    for n in range(2, bands - 1):
        ring = [(i, (i + n) % bands) for i in range(bands)]
        arrived.append(lax.ppermute(residuals[n], "lat", ring))
    first = lax.ppermute(first, "lat", even)
    second = lax.ppermute(second, "lat", odd)
    carried = 2 * per + (bands + 1) * count
    a_again, g_t, gq_t, gp_t, spread = pl.pallas_call(
        functools.partial(respond_kernel, fields, rows),
        out_shape=[line] * 5,
        in_specs=[VMEM, VMEM, HBM],
        out_specs=[VMEM] * 5,
        scratch_shapes=[tiles, pltpu.SemaphoreType.DMA((4,))],
        compiler_params=params(36),
        cost_estimate=cost(5),
        name="respond",
    )(lift, taps, a_far)
    u_t, ends = pl.pallas_call(
        functools.partial(adjoint_kernel, fields, rows),
        out_shape=[line, sds((carried, LANES))],
        in_specs=[VMEM] * (5 + len(arrived)),
        out_specs=[VMEM] * 2,
        scratch_shapes=[tiles] * 2 + [pltpu.VMEM((2, *outward.shape), BF)],
        compiler_params=params(20),
        cost_estimate=cost(3),
        name="adjoint_local",
    )(spread, first, second, a_again, g_t, *arrived)
    near_back, far_back = gather_sectors(ends)
    gradient, returned = pl.pallas_call(
        functools.partial(gradient_kernel, *sizes, count, bands),
        out_shape=[sds(flat_control.shape), sds((total, slots))],
        in_specs=[VMEM] * 8,
        out_specs=[HBM, VMEM],
        scratch_shapes=[
            tiles,
            pltpu.VMEM((rows, LANES, LANES), F32),
            pltpu.VMEM(flat_control.shape, F32),
            pltpu.SemaphoreType.DMA((fields,)),
        ],
        compiler_params=params(20),
        cost_estimate=cost(3),
        name="gradient",
    )(near, far, near_back, far_back, u_t, gq_t, gp_t, flat_control)
    return gradient.reshape(control.shape), returned[None]


def solution(mesh):
    return jax.shard_map(
        local,
        mesh=mesh,
        in_specs=(
            P(None, None, "lat", "lon"),
            P(None, None, "lat", "lon"),
            P(None, None, "lat"),
            P(),
            P(("lon", "lat"), None, None),
            P(("lon", "lat"), None),
            P(("lon", "lat"), None),
            P(("lon", "lat"), None),
            P(("lon", "lat"), None, None, None),
            P(("lon", "lat"), None, None),
            P(("lon", "lat"), None, None),
        ),
        out_specs=(P(None, None, "lat", "lon"), P(("lon", "lat"), None, None)),
        check_vma=False,
    )
```
